256 devices in a mesh: dp: 32 (over x_lo, z, core), section: 8 (over x_hi, y).
Axes of the slice: x: 4 (x_hi: 2, x_lo: 2; x = x_hi * 2 + x_lo), y: 4, z: 8, core: 2. Of those that a mesh axis runs over, the one named last changes fastest.
Arguments:
- mels: bfloat16 [24576, 128], P('dp'), may hold values from -6 to 6
- lengths: int32 [128], P('dp'), may hold values from 48 to 96, as said below
- sub_weight: bfloat16 [256, 1536], replicated, may hold values from -0.375 to 0.375
- block_weight: bfloat16 [8, 1536, 1536], P('section'), may hold values from -0.15625 to 0.15625
- conv_kernel: float32 [8, 31, 1536], P('section'), may hold values from -1 to 1
- norm_gain: float32 [8, 1536], P('section'), may hold values from 0.1 to 1.9
- cotangent: bfloat16 [12288, 1536], P('dp'), may hold values from -0.053955078 to 0.053955078
Outputs:
- weight_grad: bfloat16 [8, 1536, 1536], P('section')
- kernel_grad: float32 [8, 31, 1536], P('section')
- gain_grad: float32 [8, 1536], P('section')
The draws below stay inside these ranges and needn't reach their ends.
Inputs may be any that keep to these rules, and one draw needn't show every extreme that they name: `lengths`: frames of an utterance at or beyond its length are padding.
All inputs are finite; a program needn't handle non-finite values.
Results may differ from the reference program's by a relative error of at most 0.035.
Values may be sent and summed in bfloat16 or wider, within the bound.
No kernel may reach another device: no remote copies, remote signals or barrier semaphores. Data moves between devices by JAX's collectives and lax.ppermute only.
A program may use at most 128 MiB of HBM per device.

```python
import jax
import jax.numpy as jnp
from jax import lax

D = 1536
MELS = 128
KERNEL = 31
FRAMES = 96
TOK_DEV = 384
TOKENS = 12288
UTTS = 128
SECTIONS = 8
N_DP = 32


def draw_lengths(key, part):
    key = jax.random.fold_in(key, 11)
    values = jax.random.randint(key, (UTTS,), FRAMES // 2, FRAMES + 1)
    position = jnp.arange(UTTS)
    values = jnp.where(position == 0, FRAMES, values)
    values = jnp.where(position == 1, FRAMES // 2, values)
    return values.astype(jnp.int32)


def levels(stream_key, dims, shards, least, top_value):
    def one(dim, blocks):
        steps = jax.random.uniform(jax.random.fold_in(jax.random.fold_in(stream_key, 6), dim), (blocks,), jnp.float32, least / len(shards), top_value / len(shards))
        return jnp.repeat(jnp.exp(steps), dims[dim] // blocks).reshape((-1,) + (1,) * (len(dims) - dim - 1))

    level = one(*shards[0])
    for cut in shards[1:]:
        level = level * one(*cut)
    return level


def bell_draw(key, extent, scale, reach, cuts=(), dtype=jnp.bfloat16):
    drawn = jax.random.normal(key, extent, jnp.float32) * scale
    if len(cuts) > 0:
        drawn = levels(key, extent, cuts, -0.22, 0.18) * drawn
    return jnp.clip(drawn, min=-reach, max=reach).astype(dtype)


def setup_inputs(seed: int = 0) -> dict:
    arg_keys = jax.random.split(jax.random.key(seed), 8)
    return {
        "mels": bell_draw(arg_keys[0], (2 * TOKENS, MELS), 1.0, 6.0, ((0, 32),)),
        "lengths": draw_lengths(jax.random.fold_in(arg_keys[7], 71), 0),
        "sub_weight": bell_draw(arg_keys[2], (2 * MELS, D), (2 * MELS) ** -0.5, 0.375),
        "block_weight": bell_draw(arg_keys[3], (SECTIONS, D, D), D ** -0.5, 0.15625, ((0, 8),)),
        "conv_kernel": bell_draw(arg_keys[4], (SECTIONS, KERNEL, D), KERNEL ** -0.5, 1.0, ((0, 8),), jnp.float32),
        "norm_gain": jnp.clip(1.0 + 0.18 * jax.random.normal(arg_keys[5], (SECTIONS, D), jnp.float32), 0.1, 1.9),
        "cotangent": bell_draw(arg_keys[6], (TOKENS, D), (1.0 / (TOK_DEV * N_DP) ** 0.5), 0.053955078, ((0, 32),)),
    }


norm_eps = 1e-05

def layer_stats(block_in, gain_row, frame_mask):
    values = block_in.astype(jnp.float32)
    centre = lax.optimization_barrier(jnp.mean(values, axis=-1, keepdims=True))
    spread = lax.optimization_barrier(jnp.mean((values - centre) * (values - centre), axis=-1, keepdims=True))
    inv_std = lax.rsqrt(spread + norm_eps)
    normed = (values - centre) * inv_std
    masked = normed * gain_row * frame_mask[:, None]
    return (values, normed, inv_std, masked)

def depthwise(masked, kernel):
    width = masked.shape[-1]
    radius = kernel.shape[0] // 2
    framed = masked.reshape(-1, FRAMES, width)
    padded = jnp.pad(framed, ((0, 0), (radius, radius), (0, 0)))
    output = jnp.zeros_like(framed)
    for offset in range(kernel.shape[0]):
        output = output + kernel[offset] * padded[:, offset:offset + FRAMES]
    return output.reshape(masked.shape)

def conv_back(grad_conv, masked, kernel):
    width = masked.shape[-1]
    radius = kernel.shape[0] // 2
    framed_grad = grad_conv.reshape(-1, FRAMES, width)
    padded_grad = jnp.pad(framed_grad, ((0, 0), (radius, radius), (0, 0)))
    padded_in = jnp.pad(masked.reshape(-1, FRAMES, width), ((0, 0), (radius, radius), (0, 0)))
    grad_masked = jnp.zeros_like(framed_grad)
    kernel_rows = []
    for offset in range(kernel.shape[0]):
        start = 2 * radius - offset
        grad_masked = grad_masked + kernel[offset] * padded_grad[:, start:start + FRAMES]
        kernel_rows.append(lax.optimization_barrier(jnp.sum(framed_grad * padded_in[:, offset:offset + FRAMES], axis=(0, 1))))
    return (grad_masked.reshape(masked.shape), jnp.stack(kernel_rows))

def conv_input(block_in, kernel, gain_row, frame_mask):
    values, normed, inv_std, masked = layer_stats(block_in, gain_row, frame_mask)
    return depthwise(masked, kernel)

def section_forward(block_in, weight, kernel, gain_row, frame_mask):
    values, normed, inv_std, masked = layer_stats(block_in, gain_row, frame_mask)
    conv_out = depthwise(masked, kernel)
    hidden = jax.nn.silu(conv_out).astype(jnp.bfloat16)
    projected = jnp.dot(hidden, weight, preferred_element_type=jnp.float32)
    return ((values + projected).astype(jnp.bfloat16), conv_out)

def section_backward(grad_out, block_in, weight, kernel, gain_row, frame_mask, conv_out):
    values, normed, inv_std, masked = layer_stats(block_in, gain_row, frame_mask)
    hidden = jax.nn.silu(conv_out).astype(jnp.bfloat16)
    weight_part = lax.dot_general(hidden, grad_out, (((0,), (0,)), ((), ())), preferred_element_type=jnp.float32)
    grad_hidden = lax.dot_general(grad_out, weight, (((1,), (1,)), ((), ())), preferred_element_type=jnp.float32)
    sigma = jax.nn.sigmoid(conv_out)
    grad_conv = grad_hidden * sigma * (1.0 + conv_out * (1.0 - sigma))
    grad_masked, kernel_part = conv_back(grad_conv, masked, kernel)
    grad_normed = grad_masked * frame_mask[:, None]
    gain_part = lax.optimization_barrier(jnp.sum(grad_normed * normed, axis=0))
    scaled = grad_normed * gain_row
    grad_values = inv_std * (scaled - lax.optimization_barrier(jnp.mean(scaled, axis=-1, keepdims=True)) - normed * lax.optimization_barrier(jnp.mean(scaled * normed, axis=-1, keepdims=True)))
    grad_in = (grad_out.astype(jnp.float32) + grad_values).astype(jnp.bfloat16)
    return (grad_in, weight_part, kernel_part, gain_part)

def round_part(part):
    rounded = lax.optimization_barrier(part.astype(jnp.bfloat16))
    return rounded.astype(jnp.float32)

def reference(mels, lengths, sub_weight, block_weight, conv_kernel, norm_gain, cotangent):
    frame_mask = (jnp.arange(TOKENS) % FRAMES < jnp.repeat(lengths, FRAMES)).astype(jnp.float32)
    block_in = jnp.dot(mels.reshape(TOKENS, 2 * MELS), sub_weight, preferred_element_type=jnp.float32).astype(jnp.bfloat16)
    inputs = []
    for section_num in range(SECTIONS):
        inputs.append(block_in)
        block_in, unused = section_forward(block_in, block_weight[section_num], conv_kernel[section_num], norm_gain[section_num], frame_mask)
    grad_out = cotangent * frame_mask[:, None].astype(jnp.bfloat16)
    mask_blocks = frame_mask.reshape(N_DP, TOK_DEV)
    weight_list, kernel_list, gain_list = ([], [], [])
    for section_num in reversed(range(SECTIONS)):
        weight = block_weight[section_num]
        kernel = conv_kernel[section_num]
        gain_row = norm_gain[section_num]

        def one_block(sums, pieces):
            grad_piece, input_piece, mask_piece = pieces
            conv_out = conv_input(input_piece, kernel, gain_row, mask_piece)
            grad_in, w_part, k_part, g_part = section_backward(grad_piece, input_piece, weight, kernel, gain_row, mask_piece, conv_out)
            new_sums = (sums[0] + round_part(w_part), sums[1] + round_part(k_part), sums[2] + round_part(g_part))
            return (new_sums, grad_in)
        zeros = (jnp.zeros((D, D), jnp.float32), jnp.zeros((KERNEL, D), jnp.float32), jnp.zeros((D,), jnp.float32))
        sums, grads = lax.scan(one_block, zeros, (grad_out.reshape(N_DP, TOK_DEV, D), inputs[section_num].reshape(N_DP, TOK_DEV, D), mask_blocks))
        grad_out = grads.reshape(TOKENS, D)
        weight_list.append(sums[0].astype(jnp.bfloat16))
        kernel_list.append(sums[1])
        gain_list.append(sums[2])
    weight_grad = jnp.stack(weight_list[::-1])
    kernel_grad = jnp.stack(kernel_list[::-1])
    gain_grad = jnp.stack(gain_list[::-1])
    return (weight_grad, kernel_grad, gain_grad)
```

```python
import functools
import jax
import jax.numpy as jnp
from jax import lax
from jax.experimental import pallas as pl
from jax.experimental.pallas import tpu as pltpu
from jax.sharding import PartitionSpec as P

FRAMES = 96
EPS = 1e-05
LANES = 128
PAD = 16
TAPS = 31
BLOCK = 256
VMEM = 16 * 2**20


def taps_sum(padded, taps, tile, reverse):
    total = None
    for low in range(8):
        shifted = padded[tile, pl.ds(low, FRAMES + 24), :]
        for high in range(4):
            j = 8 * high + low - 1
            if 0 <= j < TAPS:
                row = TAPS - 1 - j if reverse else j
                tap = taps[row : row + 1, tile * LANES : (tile + 1) * LANES]
                term = tap * shifted[8 * high : 8 * high + FRAMES]
                total = term if total is None else total + term
    return total


def clear_rims(padded):
    rim = jnp.zeros((padded.shape[0], PAD, LANES), jnp.float32)
    padded[:, 0:PAD, :] = rim
    padded[:, PAD + FRAMES :, :] = rim


def frame_rows(length):
    rows = lax.broadcasted_iota(jnp.int32, (FRAMES, LANES), 0)
    return (rows < length).astype(jnp.float32)


def forward_kernel(tick, info, recv, subs, weight, taps, gain, *rest):
    out, conv_all, norm_all, inv_all, hid_all, block_in, padded, total = rest[-8:]
    section = info[0]
    slot = tick - 2 * section
    width = out.shape[1]
    tiles = width // LANES

    @pl.when((slot >= 0) & (slot < subs.shape[0]))
    def _():
        @pl.when(section == 0)
        def _():
            block_in[...] = subs[slot]

        @pl.when(section != 0)
        def _():
            block_in[...] = recv[...]

        clear_rims(padded)
        mask = frame_rows(info[1 + slot])
        sums = jnp.zeros((FRAMES, LANES), jnp.float32)
        for tile in range(tiles):
            cols = slice(tile * LANES, (tile + 1) * LANES)
            sums = sums + block_in[:, cols].astype(jnp.float32)
        centre = jnp.sum(sums, axis=1, keepdims=True) * (1.0 / width)
        sums = jnp.zeros((FRAMES, LANES), jnp.float32)
        for tile in range(tiles):
            cols = slice(tile * LANES, (tile + 1) * LANES)
            gap = block_in[:, cols].astype(jnp.float32) - centre
            sums = sums + gap * gap
        spread = jnp.sum(sums, axis=1, keepdims=True) * (1.0 / width)
        inv_std = jnp.broadcast_to(lax.rsqrt(spread + EPS), (FRAMES, LANES))
        centre = jnp.broadcast_to(centre, (FRAMES, LANES))
        inv_all[slot] = inv_std
        for chunk in range(width // BLOCK):
            hidden = []
            for tile in range(chunk * BLOCK // LANES, (chunk + 1) * BLOCK // LANES):
                cols = slice(tile * LANES, (tile + 1) * LANES)
                normed = (block_in[:, cols].astype(jnp.float32) - centre) * inv_std
                norm_all[slot, :, cols] = normed
                padded[tile, PAD : PAD + FRAMES, :] = normed * gain[:, cols] * mask
                conv = taps_sum(padded, taps, tile, False)
                conv_all[slot, :, cols] = conv
                hidden.append((conv / (1.0 + jnp.exp(-conv))).astype(jnp.bfloat16))
            hidden = jnp.concatenate(hidden, axis=1)
            rows = slice(chunk * BLOCK, (chunk + 1) * BLOCK)
            hid_all[slot, :, rows] = hidden
            part = jnp.dot(hidden, weight[rows, :], preferred_element_type=jnp.float32)
            if chunk == 0:
                total[...] = part
            else:
                total[...] += part
        out[...] = (block_in[...].astype(jnp.float32) + total[...]).astype(jnp.bfloat16)


def forward_call(tick, info, recv, subs, weight, taps, gain, stash):
    groups, _, width = subs.shape
    f32, bf16 = jnp.float32, jnp.bfloat16
    shapes = (
        jax.ShapeDtypeStruct((FRAMES, width), bf16),
        jax.ShapeDtypeStruct((groups, FRAMES, width), f32),
        jax.ShapeDtypeStruct((groups, FRAMES, width), f32),
        jax.ShapeDtypeStruct((groups, FRAMES, LANES), f32),
        jax.ShapeDtypeStruct((groups, FRAMES, width), bf16),
    )
    smem = pl.BlockSpec(memory_space=pltpu.SMEM)
    vmem = pl.BlockSpec(memory_space=pltpu.VMEM)
    held = () if stash is None else tuple(stash)
    res = pl.pallas_call(
        functools.partial(forward_kernel, tick),
        out_shape=shapes,
        in_specs=[smem] + [vmem] * (5 + len(held)),
        out_specs=(vmem,) * 5,
        scratch_shapes=[
            pltpu.VMEM((FRAMES, width), bf16),
            pltpu.VMEM((width // LANES, FRAMES + 2 * PAD, LANES), f32),
            pltpu.VMEM((FRAMES, width), f32),
        ],
        input_output_aliases={6 + i: 1 + i for i in range(len(held))},
        compiler_params=pltpu.CompilerParams(vmem_limit_bytes=VMEM),
        cost_estimate=pl.CostEstimate(
            flops=8 * FRAMES * width * width, bytes_accessed=width * width * 2, transcendentals=0
        ),
        name="section_forward",
    )(info, recv, subs, weight, taps, gain, *held)
    return res[0], res[1:]


def backward_kernel(tick, sections, info, recv, seeds, weight, taps, gain, conv_all, norm_all, inv_all, *rest):
    out, grad_all, gconv_all, gain_all, grad_out, padded, scaled_now = rest[-7:]
    section = info[0]
    slot = tick - 2 * (sections - 1 - section)
    width = out.shape[1]
    tiles = width // LANES

    @pl.when((slot >= 0) & (slot < seeds.shape[0]))
    def _():
        mask = frame_rows(info[1 + slot])

        @pl.when(section == sections - 1)
        def _():
            for tile in range(tiles):
                cols = slice(tile * LANES, (tile + 1) * LANES)
                grad_out[:, cols] = (seeds[slot, :, cols].astype(jnp.float32) * mask).astype(
                    jnp.bfloat16
                )

        @pl.when(section != sections - 1)
        def _():
            grad_out[...] = recv[...]

        clear_rims(padded)
        grad_all[slot] = grad_out[...]
        mean_sum = jnp.zeros((FRAMES, LANES), jnp.float32)
        dot_sum = jnp.zeros((FRAMES, LANES), jnp.float32)
        for chunk in range(width // BLOCK):
            rows = slice(chunk * BLOCK, (chunk + 1) * BLOCK)
            grad_hidden = lax.dot_general(
                grad_out[...], weight[rows, :], (((1,), (1,)), ((), ())),
                preferred_element_type=jnp.float32,
            )
            for step in range(BLOCK // LANES):
                tile = chunk * BLOCK // LANES + step
                cols = slice(tile * LANES, (tile + 1) * LANES)
                conv = conv_all[slot, :, cols]
                sigma = 1.0 / (1.0 + jnp.exp(-conv))
                gconv = grad_hidden[:, step * LANES : (step + 1) * LANES] * sigma * (
                    1.0 + conv * (1.0 - sigma)
                )
                gconv_all[slot, :, cols] = gconv
                padded[tile, PAD : PAD + FRAMES, :] = gconv
                grad_normed = taps_sum(padded, taps, tile, True) * mask
                normed = norm_all[slot, :, cols]
                product = grad_normed * normed
                part = product[0:8]
                for row in range(8, FRAMES, 8):
                    part = part + product[row : row + 8]
                gain_all[slot, :, cols] = part
                scaled = grad_normed * gain[:, cols]
                scaled_now[:, cols] = scaled
                mean_sum = mean_sum + scaled
                dot_sum = dot_sum + scaled * normed
        mean_row = jnp.sum(mean_sum, axis=1, keepdims=True) * (1.0 / width)
        dot_row = jnp.sum(dot_sum, axis=1, keepdims=True) * (1.0 / width)
        mean_row = jnp.broadcast_to(mean_row, (FRAMES, LANES))
        dot_row = jnp.broadcast_to(dot_row, (FRAMES, LANES))
        inv_std = inv_all[slot]
        for tile in range(tiles):
            cols = slice(tile * LANES, (tile + 1) * LANES)
            change = inv_std * (scaled_now[:, cols] - mean_row - norm_all[slot, :, cols] * dot_row)
            out[:, cols] = (grad_out[:, cols].astype(jnp.float32) + change).astype(jnp.bfloat16)


def backward_call(tick, sections, info, recv, seeds, weight, taps, gain, stash, held):
    groups, _, width = seeds.shape
    f32, bf16 = jnp.float32, jnp.bfloat16
    shapes = (
        jax.ShapeDtypeStruct((FRAMES, width), bf16),
        jax.ShapeDtypeStruct((groups, FRAMES, width), bf16),
        jax.ShapeDtypeStruct((groups, FRAMES, width), f32),
        jax.ShapeDtypeStruct((groups, 8, width), f32),
    )
    smem = pl.BlockSpec(memory_space=pltpu.SMEM)
    vmem = pl.BlockSpec(memory_space=pltpu.VMEM)
    held = () if held is None else tuple(held)
    res = pl.pallas_call(
        functools.partial(backward_kernel, tick, sections),
        out_shape=shapes,
        in_specs=[smem] + [vmem] * (8 + len(held)),
        out_specs=(vmem,) * 4,
        scratch_shapes=[
            pltpu.VMEM((FRAMES, width), bf16),
            pltpu.VMEM((width // LANES, FRAMES + 2 * PAD, LANES), f32),
            pltpu.VMEM((FRAMES, width), f32),
        ],
        input_output_aliases={9 + i: 1 + i for i in range(len(held))},
        compiler_params=pltpu.CompilerParams(vmem_limit_bytes=VMEM),
        cost_estimate=pl.CostEstimate(
            flops=8 * FRAMES * width * width, bytes_accessed=width * width * 2, transcendentals=0
        ),
        name="section_backward",
    )(info, recv, seeds, weight, taps, gain, *stash[:3], *held)
    return res[0], res[1:]


def taps_kernel(info, gconv, norm, gain, out, padded):
    groups = gconv.shape[0]
    sums = [jnp.zeros((8, LANES), jnp.float32) for _ in range(TAPS)]
    clear_rims(padded)
    for group in range(groups):
        mask = frame_rows(info[1 + group])
        padded[0, PAD : PAD + FRAMES, :] = norm[group] * gain[...] * mask
        grads = gconv[group]
        for low in range(8):
            shifted = padded[0, pl.ds(low, FRAMES + 24), :]
            for high in range(4):
                j = 8 * high + low - 1
                if 0 <= j < TAPS:
                    product = grads * shifted[8 * high : 8 * high + FRAMES]
                    part = product[0:8]
                    for row in range(8, FRAMES, 8):
                        part = part + product[row : row + 8]
                    sums[j] = sums[j] + part
    for j in range(TAPS):
        out[j : j + 1, :] = jnp.sum(sums[j], axis=0, keepdims=True)
    out[TAPS : TAPS + 1, :] = jnp.zeros((1, LANES), jnp.float32)


def taps_call(info, gconv, norm, gain):
    groups, _, width = gconv.shape
    block = pl.BlockSpec((groups, FRAMES, LANES), lambda i: (0, 0, i))
    return pl.pallas_call(
        taps_kernel,
        grid=(width // LANES,),
        out_shape=jax.ShapeDtypeStruct((TAPS + 1, width), jnp.float32),
        in_specs=[
            pl.BlockSpec(memory_space=pltpu.SMEM),
            block,
            block,
            pl.BlockSpec((1, LANES), lambda i: (0, i)),
        ],
        out_specs=pl.BlockSpec((TAPS + 1, LANES), lambda i: (0, i)),
        scratch_shapes=[pltpu.VMEM((1, FRAMES + 2 * PAD, LANES), jnp.float32)],
        compiler_params=pltpu.CompilerParams(vmem_limit_bytes=VMEM),
        name="taps_gradient",
    )(info, gconv, norm, gain)


def column_sum(rows, small, shards):
    half_rows, width = rows.shape[0] // 2, rows.shape[1]
    ring = shards // 4
    cut = half_rows // ring
    extra = (TAPS + 1) // 2 // ring
    shard = lax.axis_index("dp")
    core, place = shard % 2, (shard // 2) % ring
    f32, bf16 = jnp.float32, jnp.bfloat16

    def along_z(block, step):
        route = []
        for d in range(shards):
            x, z, c = d // (2 * ring), (d // 2) % ring, d % 2
            route.append((d, (x * ring + (z + step) % ring) * 2 + c))
        return lax.ppermute(block, "dp", route)

    def to_core(block):
        return lax.ppermute(block, "dp", [(d, d ^ 1) for d in range(shards)])

    def to_x(block):
        return lax.ppermute(block, "dp", [(d, (d + shards // 2) % shards) for d in range(shards)])

    def add(*terms):
        total = terms[0].astype(f32)
        for term in terms[1:]:
            total = total + term.astype(f32)
        return total.astype(bf16)

    halves = rows.reshape(2, half_rows, width)
    swapped = to_core(lax.dynamic_index_in_dim(halves, 1 - core, 0, False))
    mine = add(lax.dynamic_index_in_dim(halves, core, 0, False), swapped)
    small_now = small()
    small_halves = small_now.reshape(2, ring * extra, width)
    small_swapped = to_core(lax.dynamic_index_in_dim(small_halves, 1 - core, 0, False))
    small_mine = add(lax.dynamic_index_in_dim(small_halves, core, 0, False), small_swapped)
    pad = 8 - extra
    parts = jnp.concatenate(
        [
            mine.reshape(ring, cut, width),
            small_mine.reshape(ring, extra, width),
            jnp.zeros((ring, pad, width), bf16),
        ],
        axis=1,
    )

    def local(owner):
        return lax.dynamic_index_in_dim(parts, owner % ring, 0, False)

    ahead, behind = ring // 2, ring - 1 - ring // 2
    up = along_z(local(place + ahead), 1)
    down = along_z(local(place + ring - behind), -1)
    for step in range(1, ahead):
        up = along_z(add(up, local(place + ahead - step)), 1)
        if step < behind:
            down = along_z(add(down, local(place + ring - behind + step)), -1)
    done = add(local(place), up, down)
    done = add(done, to_x(done))

    whole = jnp.zeros((2, ring, cut, width), bf16)
    edge = jnp.zeros((2, ring, extra, width), bf16)

    def put(whole, edge, block, owner, side):
        start = (side, owner % ring, 0, 0)
        whole = lax.dynamic_update_slice(whole, block[None, None, :cut], start)
        edge = lax.dynamic_update_slice(edge, block[None, None, cut : cut + extra], start)
        return whole, edge

    up = down = done
    whole, edge = put(whole, edge, done, place, core)
    other = to_core(done)
    whole, edge = put(whole, edge, other, place, 1 - core)
    for step in range(1, ahead + 1):
        up = along_z(up, 1)
        arrived = [(up, place + ring - step)]
        if step <= behind:
            down = along_z(down, -1)
            arrived.append((down, place + step))
        for block, owner in arrived:
            other = to_core(block)
            whole, edge = put(whole, edge, block, owner, core)
            whole, edge = put(whole, edge, other, owner, 1 - core)
    return whole.reshape(rows.shape), edge.reshape(small_now.shape)


def body(mels, lengths, sub_weight, block_weight, conv_kernel, norm_gain, cotangent):
    weight = block_weight[0]
    taps = conv_kernel[0]
    gain = norm_gain
    width = cotangent.shape[1]
    groups = lengths.shape[0]
    sections = lax.axis_size("section")
    shards = lax.axis_size("dp")
    section_idx = lax.axis_index("section")
    crossing = sections // 2

    def flip(shard):
        return (shard + shards // 2) % shards

    def linear(shard, section):
        return shard * sections + section

    def relay(block, pairs):
        route = []
        for source, target in pairs:
            crossed = (source < crossing) != (target < crossing)
            for shard in range(shards):
                there = flip(shard) if crossed else shard
                route.append((linear(shard, source), linear(there, target)))
        return lax.ppermute(block, ("dp", "section"), route)

    upper = range(crossing, sections)
    lens_flipped = lax.ppermute(
        lengths,
        ("dp", "section"),
        [(linear(d, s), linear(flip(d), s)) for d in range(shards) for s in upper],
    )
    lens = jnp.where(section_idx >= crossing, lens_flipped, lengths)
    seeds = lax.ppermute(
        cotangent,
        ("dp", "section"),
        [(linear(d, sections - 1), linear(flip(d), sections - 1)) for d in range(shards)],
    ).reshape(groups, FRAMES, width)
    subs = (
        jnp.dot(
            mels.reshape(groups * FRAMES, -1), sub_weight, preferred_element_type=jnp.float32
        )
        .astype(jnp.bfloat16)
        .reshape(groups, FRAMES, width)
    )
    info = jnp.concatenate([section_idx.astype(jnp.int32).reshape(1), lens])
    turn = 2 * (sections - 1)
    ticks = turn + groups
    stash = held = None
    fwd_recv = {}
    bwd_recv = {}
    idle = jnp.zeros((FRAMES, width), jnp.bfloat16)
    for tick in range(turn + ticks):
        if tick < ticks:
            block, stash = forward_call(
                tick, info, fwd_recv.pop(tick - 2, idle), subs, weight, taps, gain, stash
            )
            pairs = [(s, s + 1) for s in range(sections - 1) if 0 <= tick - 2 * s < groups]
            if pairs:
                fwd_recv[tick] = relay(block, pairs)
        back = tick - turn
        if back >= 0:
            block, held = backward_call(
                back, sections, info, bwd_recv.pop(back - 2, idle), seeds, weight, taps, gain, stash, held
            )
            pairs = [
                (s, s - 1)
                for s in range(1, sections)
                if 0 <= back - 2 * (sections - 1 - s) < groups
            ]
            if pairs:
                bwd_recv[back] = relay(block, pairs)
    rows = groups * FRAMES
    part = lax.dot_general(
        stash[3].reshape(rows, width),
        held[0].reshape(rows, width),
        (((0,), (0,)), ((), ())),
        preferred_element_type=jnp.float32,
    ).astype(jnp.bfloat16)

    def small():
        rows = taps_call(info, held[1], stash[1], gain)
        return rows.at[TAPS].set(jnp.sum(held[2], axis=(0, 1))).astype(jnp.bfloat16)

    part, edge = column_sum(part, small, shards)
    edge = edge.astype(jnp.float32)
    return (part[None], edge[None, :TAPS], edge[None, TAPS])


def solution(mesh):
    return jax.shard_map(
        body,
        mesh=mesh,
        in_specs=(
            P("dp", None),
            P("dp"),
            P(),
            P("section", None, None),
            P("section", None, None),
            P("section", None),
            P("dp", None),
        ),
        out_specs=(P("section", None, None), P("section", None, None), P("section", None)),
        check_vma=False,
    )
```

```python
import functools
import jax
import jax.numpy as jnp
from jax import lax
from jax.experimental import pallas as pl
from jax.experimental.pallas import tpu as pltpu
from jax.sharding import PartitionSpec as P

FRAMES = 96
EPS = 1e-05
LANES = 128
PAD = 16
TAPS = 31
BLOCK = 256
VMEM = 16 * 2**20


def taps_sum(padded, taps, cols, reverse):
    total = None
    for low in range(8):
        shifted = padded[pl.ds(low, FRAMES + 24), :]
        for high in range(4):
            j = 8 * high + low - 1
            if 0 <= j < TAPS:
                row = TAPS - 1 - j if reverse else j
                term = taps[row : row + 1, cols] * shifted[8 * high : 8 * high + FRAMES]
                total = term if total is None else total + term
    return total


def lane_tile(tile):
    return pl.ds(pl.multiple_of(tile * LANES, LANES), LANES)


def lane_block(chunk):
    return pl.ds(pl.multiple_of(chunk * BLOCK, BLOCK), BLOCK)


def clear_rims(padded):
    rim = jnp.zeros((padded.shape[0], PAD, LANES), jnp.float32)
    padded[:, 0:PAD, :] = rim
    padded[:, PAD + FRAMES :, :] = rim


def frame_rows(length):
    rows = lax.broadcasted_iota(jnp.int32, (FRAMES, LANES), 0)
    return (rows < length).astype(jnp.float32)


def forward_kernel(tick, info, recv, subs, weight, taps, gain, *rest):
    out, conv_all, norm_all, inv_all, hid_all, block_in, padded, total = rest[-8:]
    section = info[0]
    slot = tick - section
    width = out.shape[1]
    tiles = width // LANES
    chunks = width // BLOCK
    zeros = jnp.zeros((FRAMES, LANES), jnp.float32)

    @pl.when((slot >= 0) & (slot < subs.shape[0]))
    def _():
        @pl.when(section == 0)
        def _():
            block_in[...] = subs[slot]

        @pl.when(section != 0)
        def _():
            block_in[...] = recv[...]

        clear_rims(padded)
        mask = frame_rows(info[1 + slot])

        def add_up(tile, sums):
            return sums + block_in[:, lane_tile(tile)].astype(jnp.float32)

        centre = jnp.sum(lax.fori_loop(0, tiles, add_up, zeros, unroll=4), axis=1, keepdims=True)
        centre = jnp.broadcast_to(centre * (1.0 / width), (FRAMES, LANES))

        def add_squares(tile, sums):
            gap = block_in[:, lane_tile(tile)].astype(jnp.float32) - centre
            return sums + gap * gap

        spread = jnp.sum(
            lax.fori_loop(0, tiles, add_squares, zeros, unroll=4), axis=1, keepdims=True
        )
        inv_std = jnp.broadcast_to(lax.rsqrt(spread * (1.0 / width) + EPS), (FRAMES, LANES))
        inv_all[slot] = inv_std
        total[...] = block_in[...].astype(jnp.float32)
        hid_all[slot, :, 0:BLOCK] = jnp.zeros((FRAMES, BLOCK), jnp.bfloat16)

        def project(chunk):
            cols = lane_block(chunk)
            total[...] += jnp.dot(
                hid_all[slot, :, cols], weight[cols, :], preferred_element_type=jnp.float32
            )

        def one_chunk(chunk, carry):
            project(jnp.maximum(chunk - 1, 0))
            for step in range(BLOCK // LANES):
                cols = lane_tile(chunk * (BLOCK // LANES) + step)
                normed = (block_in[:, cols].astype(jnp.float32) - centre) * inv_std
                norm_all[slot, :, cols] = normed
                padded[step, PAD : PAD + FRAMES, :] = normed * gain[:, cols] * mask
                conv = taps_sum(padded.at[step], taps, cols, False)
                conv_all[slot, :, cols] = conv
                hid_all[slot, :, cols] = (conv / (1.0 + jnp.exp(-conv))).astype(jnp.bfloat16)
            return carry

        lax.fori_loop(0, chunks, one_chunk, 0)
        project(chunks - 1)
        out[...] = total[...].astype(jnp.bfloat16)


def forward_call(tick, info, recv, subs, weight, taps, gain, stash):
    groups, _, width = subs.shape
    f32, bf16 = jnp.float32, jnp.bfloat16
    shapes = (
        jax.ShapeDtypeStruct((FRAMES, width), bf16),
        jax.ShapeDtypeStruct((groups, FRAMES, width), f32),
        jax.ShapeDtypeStruct((groups, FRAMES, width), f32),
        jax.ShapeDtypeStruct((groups, FRAMES, LANES), f32),
        jax.ShapeDtypeStruct((groups, FRAMES, width), bf16),
    )
    smem = pl.BlockSpec(memory_space=pltpu.SMEM)
    vmem = pl.BlockSpec(memory_space=pltpu.VMEM)
    held = () if stash is None else tuple(stash)
    res = pl.pallas_call(
        functools.partial(forward_kernel, tick),
        out_shape=shapes,
        in_specs=[smem] + [vmem] * (5 + len(held)),
        out_specs=(vmem,) * 5,
        scratch_shapes=[
            pltpu.VMEM((FRAMES, width), bf16),
            pltpu.VMEM((BLOCK // LANES, FRAMES + 2 * PAD, LANES), f32),
            pltpu.VMEM((FRAMES, width), f32),
        ],
        input_output_aliases={6 + i: 1 + i for i in range(len(held))},
        compiler_params=pltpu.CompilerParams(vmem_limit_bytes=VMEM),
        cost_estimate=pl.CostEstimate(
            flops=8 * FRAMES * width * width, bytes_accessed=width * width * 2, transcendentals=0
        ),
        name="section_forward",
    )(info, recv, subs, weight, taps, gain, *held)
    return res[0], res[1:]


def backward_kernel(tick, sections, info, recv, seeds, weight, taps, gain, conv_all, norm_all, inv_all, *rest):
    out, grad_all, gconv_all, gain_all = rest[-10:-6]
    grad_out, padded, scaled_now, ahead, mean_sum, dot_sum = rest[-6:]
    section = info[0]
    slot = tick - (sections - 1 - section)
    width = out.shape[1]
    tiles = width // LANES
    chunks = width // BLOCK

    @pl.when((slot >= 0) & (slot < seeds.shape[0]))
    def _():
        mask = frame_rows(info[1 + slot])

        @pl.when(section == sections - 1)
        def _():
            def seed(tile, carry):
                cols = lane_tile(tile)
                masked = seeds[slot, :, cols].astype(jnp.float32) * mask
                grad_out[:, cols] = masked.astype(jnp.bfloat16)
                return carry

            lax.fori_loop(0, tiles, seed, 0)

        @pl.when(section != sections - 1)
        def _():
            grad_out[...] = recv[...]

        clear_rims(padded)
        grad_all[slot] = grad_out[...]
        mean_sum[...] = jnp.zeros((FRAMES, LANES), jnp.float32)
        dot_sum[...] = jnp.zeros((FRAMES, LANES), jnp.float32)

        def back_project(chunk):
            return lax.dot_general(
                grad_out[...],
                weight[lane_block(chunk), :],
                (((1,), (1,)), ((), ())),
                preferred_element_type=jnp.float32,
            )

        ahead[0] = back_project(0)

        def one_chunk(chunk, carry):
            grad_hidden = ahead[chunk % 2]
            ahead[(chunk + 1) % 2] = back_project(jnp.minimum(chunk + 1, chunks - 1))
            for step in range(BLOCK // LANES):
                cols = lane_tile(chunk * (BLOCK // LANES) + step)
                conv = conv_all[slot, :, cols]
                sigma = 1.0 / (1.0 + jnp.exp(-conv))
                gconv = grad_hidden[:, step * LANES : (step + 1) * LANES] * sigma * (
                    1.0 + conv * (1.0 - sigma)
                )
                gconv_all[slot, :, cols] = gconv
                padded[step, PAD : PAD + FRAMES, :] = gconv
                grad_normed = taps_sum(padded.at[step], taps, cols, True) * mask
                normed = norm_all[slot, :, cols]
                product = grad_normed * normed
                part = product[0:8]
                for row in range(8, FRAMES, 8):
                    part = part + product[row : row + 8]
                gain_all[slot, :, cols] = part
                scaled = grad_normed * gain[:, cols]
                scaled_now[:, cols] = scaled
                mean_sum[...] += scaled
                dot_sum[...] += scaled * normed
            return carry

        lax.fori_loop(0, chunks, one_chunk, 0)
        mean_row = jnp.sum(mean_sum[...], axis=1, keepdims=True) * (1.0 / width)
        dot_row = jnp.sum(dot_sum[...], axis=1, keepdims=True) * (1.0 / width)
        mean_row = jnp.broadcast_to(mean_row, (FRAMES, LANES))
        dot_row = jnp.broadcast_to(dot_row, (FRAMES, LANES))
        inv_std = inv_all[slot]

        def finish(tile, carry):
            cols = lane_tile(tile)
            change = inv_std * (scaled_now[:, cols] - mean_row - norm_all[slot, :, cols] * dot_row)
            out[:, cols] = (grad_out[:, cols].astype(jnp.float32) + change).astype(jnp.bfloat16)
            return carry

        lax.fori_loop(0, tiles, finish, 0, unroll=2)


def backward_call(tick, sections, info, recv, seeds, weight, taps, gain, stash, held):
    groups, _, width = seeds.shape
    f32, bf16 = jnp.float32, jnp.bfloat16
    shapes = (
        jax.ShapeDtypeStruct((FRAMES, width), bf16),
        jax.ShapeDtypeStruct((groups, FRAMES, width), bf16),
        jax.ShapeDtypeStruct((groups, FRAMES, width), f32),
        jax.ShapeDtypeStruct((groups, 8, width), f32),
    )
    smem = pl.BlockSpec(memory_space=pltpu.SMEM)
    vmem = pl.BlockSpec(memory_space=pltpu.VMEM)
    held = () if held is None else tuple(held)
    res = pl.pallas_call(
        functools.partial(backward_kernel, tick, sections),
        out_shape=shapes,
        in_specs=[smem] + [vmem] * (8 + len(held)),
        out_specs=(vmem,) * 4,
        scratch_shapes=[
            pltpu.VMEM((FRAMES, width), bf16),
            pltpu.VMEM((BLOCK // LANES, FRAMES + 2 * PAD, LANES), f32),
            pltpu.VMEM((FRAMES, width), f32),
            pltpu.VMEM((2, FRAMES, BLOCK), f32),
            pltpu.VMEM((FRAMES, LANES), f32),
            pltpu.VMEM((FRAMES, LANES), f32),
        ],
        input_output_aliases={9 + i: 1 + i for i in range(len(held))},
        compiler_params=pltpu.CompilerParams(vmem_limit_bytes=VMEM),
        cost_estimate=pl.CostEstimate(
            flops=8 * FRAMES * width * width, bytes_accessed=width * width * 2, transcendentals=0
        ),
        name="section_backward",
    )(info, recv, seeds, weight, taps, gain, *stash[:3], *held)
    return res[0], res[1:]


def taps_kernel(tick, sections, info, gconv_all, norm_all, gain, gain_all, *rest):
    out, padded = rest[-2:]
    slot = tick - (sections - 1 - info[0])
    width = out.shape[1]
    if len(rest) == 2:
        out[...] = jnp.zeros(out.shape, jnp.float32)

    @pl.when((slot >= 0) & (slot < gconv_all.shape[0]))
    def _():
        mask = frame_rows(info[1 + slot])
        clear_rims(padded)

        def one_tile(tile, carry):
            cols = lane_tile(tile)
            padded[0, PAD : PAD + FRAMES, :] = norm_all[slot, :, cols] * gain[:, cols] * mask
            grads = gconv_all[slot, :, cols]
            for low in range(8):
                shifted = padded[0, pl.ds(low, FRAMES + 24), :]
                for high in range(4):
                    j = 8 * high + low - 1
                    if 0 <= j < TAPS:
                        product = grads * shifted[8 * high : 8 * high + FRAMES]
                        part = product[0:8]
                        for row in range(8, FRAMES, 8):
                            part = part + product[row : row + 8]
                        out[j : j + 1, cols] += jnp.sum(part, axis=0, keepdims=True)
            out[TAPS : TAPS + 1, cols] += jnp.sum(gain_all[slot, :, cols], axis=0, keepdims=True)
            return carry

        lax.fori_loop(0, width // LANES, one_tile, 0)


def on_chip(kernel, name, shapes, operands, scratch=(), aliases=None, flops=10**9, hbm_out=()):
    vmem = pl.BlockSpec(memory_space=pltpu.VMEM)
    smem = pl.BlockSpec(memory_space=pltpu.SMEM)
    anywhere = pl.BlockSpec(memory_space=pl.ANY)
    aliases = aliases or {}
    return pl.pallas_call(
        kernel,
        out_shape=tuple(jax.ShapeDtypeStruct(shape, dtype) for shape, dtype in shapes),
        in_specs=[smem]
        + [anywhere if aliases.get(i + 1) in hbm_out else vmem for i in range(len(operands) - 1)],
        out_specs=tuple(anywhere if i in hbm_out else vmem for i in range(len(shapes))),
        scratch_shapes=list(scratch),
        input_output_aliases=aliases,
        compiler_params=pltpu.CompilerParams(vmem_limit_bytes=VMEM),
        cost_estimate=pl.CostEstimate(flops=flops, bytes_accessed=2**20, transcendentals=0),
        name=name,
    )(*operands)


def taps_call(tick, sections, info, held, stash, gain, sums):
    width = gain.shape[1]
    operands = (info, held[1], stash[1], gain, held[2]) + (() if sums is None else (sums,))
    return on_chip(
        functools.partial(taps_kernel, tick, sections),
        "taps_gradient",
        [((TAPS + 1, width), jnp.float32)],
        operands,
        [pltpu.VMEM((1, FRAMES + 2 * PAD, LANES), jnp.float32)],
        {} if sums is None else {5: 0},
    )[0]


EXTRA = 8


def part_kernel(own, info, hid_all, grad_all, sums, out):
    ring, sides, rows, width = out.shape
    cut = rows - EXTRA
    half = info[5] if own else 1 - info[5]
    piece = 8 * cut
    tokens = hid_all.shape[0] * FRAMES
    grads = grad_all[...].reshape(tokens, width)
    for step in range(ring * sides * cut // piece):
        start = pl.multiple_of(half * (ring * sides * cut) + step * piece, LANES)
        hidden = hid_all[:, :, pl.ds(start, piece)].reshape(tokens, piece)
        part = lax.dot_general(
            hidden, grads, (((0,), (0,)), ((), ())), preferred_element_type=jnp.float32
        )
        for i in range(piece // cut):
            block = step * (piece // cut) + i
            out[block // sides, block % sides, 0:cut] = part[i * cut : (i + 1) * cut].astype(
                jnp.bfloat16
            )
    rest = jnp.zeros((EXTRA - 1, width), jnp.float32)
    for block in range(ring * sides):
        row = sums[pl.ds(half * (ring * sides) + block, 1), :]
        out[block // sides, block % sides, cut:] = jnp.concatenate([row, rest], axis=0).astype(
            jnp.bfloat16
        )


def merge_kernel(info, mine, other, own, *sends):
    ring = mine.shape[0]
    place, side = info[6], info[7]
    ahead, behind = ring // 2, ring - 1 - ring // 2

    def add(owner, x):
        owner = owner % ring
        return (mine[owner, x].astype(jnp.float32) + other[owner, x].astype(jnp.float32)).astype(
            jnp.bfloat16
        )

    for step, send in enumerate(sends):
        send[0] = add(place + ahead - step, 1 - side)
        send[1] = add(place + ring - behind + step, 1 - side)
    for owner in range(ring):
        own[owner] = add(owner, side)


def ring_kernel(step, info, own, crossed, *rest):
    ring = own.shape[0]
    place = info[6]
    ahead, behind = ring // 2, ring - 1 - ring // 2
    up = own[(place + ahead - step) % ring].astype(jnp.float32) + crossed[0].astype(jnp.float32)
    down = own[(place + ring - behind + step) % ring].astype(jnp.float32) + crossed[1].astype(
        jnp.float32
    )
    if len(rest) == 4:
        up = up + rest[0][...].astype(jnp.float32)
        down = down + rest[1][...].astype(jnp.float32)
    rest[-2][...] = up.astype(rest[-2].dtype)
    rest[-1][...] = down.astype(rest[-1].dtype)


def place_kernel(ring, sources, count, info, *rest):
    blocks = rest[:count]
    whole, edge, sems = rest[-3:]
    core, place, side = info[5], info[6], info[7]
    cut = blocks[0].shape[-2] - EXTRA
    copies = []
    for n, (which, i, offset, core_flip, side_flip) in enumerate(sources):
        block = blocks[which] if i is None else blocks[which].at[i]
        half = 1 - core if core_flip else core
        x = 1 - side if side_flip else side
        index = (half * ring + (place + offset + ring) % ring) * 2 + x
        start = pl.multiple_of(index * cut, cut)
        copy = pltpu.make_async_copy(
            block.at[pl.ds(0, cut)], whole.at[pl.ds(start, cut)], sems.at[n]
        )
        copy.start()
        copies.append(copy)
        edge[index] = block[cut:, :].astype(jnp.float32)
    for copy in copies:
        copy.wait()


def place_call(info, pieces, shape, ring, held):
    blocks, sources = [], []
    for block, i, offset, core_flip, side_flip in pieces:
        which = [n for n, other in enumerate(blocks) if other is block]
        if not which:
            which = [len(blocks)]
            blocks.append(block)
        sources.append((which[0], i, offset, core_flip, side_flip))
    count = len(blocks)
    return on_chip(
        functools.partial(place_kernel, ring, sources, count),
        "place_sums",
        [(shape, jnp.bfloat16), ((4 * ring, EXTRA, shape[1]), jnp.float32)],
        (info, *blocks, *(held or ())),
        [pltpu.SemaphoreType.DMA((len(sources),))],
        {count + 1: 0, count + 2: 1} if held else {},
        hbm_out=(0,),
    )


def column_sum(info, hidden, grads, sums, shards):
    ring = shards // 4
    width = grads.shape[2]
    cut = width // shards
    rows = cut + EXTRA
    f32, bf16 = jnp.float32, jnp.bfloat16

    def along_z(block, step):
        route = []
        for d in range(shards):
            x, z, c = d // (2 * ring), (d // 2) % ring, d % 2
            route.append((d, (x * ring + (z + step) % ring) * 2 + c))
        return lax.ppermute(block, "dp", route)

    def to_core(block):
        return lax.ppermute(block, "dp", [(d, d ^ 1) for d in range(shards)])

    def to_x(block):
        return lax.ppermute(block, "dp", [(d, (d + shards // 2) % shards) for d in range(shards)])

    def part(own):
        return on_chip(
            functools.partial(part_kernel, own),
            "weight_part",
            [((ring, 2, rows, width), bf16)],
            (info, hidden, grads, sums),
            flops=4 * 10**9,
        )[0]

    swapped = to_core(part(False))
    mine = part(True)
    ahead, behind = ring // 2, ring - 1 - ring // 2
    merged = on_chip(
        merge_kernel,
        "merge_cores",
        [((ring, rows, width), bf16)] + [((2, rows, width), bf16)] * ahead,
        (info, mine, swapped),
    )
    own, crossed = merged[0], [to_x(send) for send in merged[1:]]
    up = down = None
    for step in range(ahead):
        arrived = () if step == 0 else (up, down)
        last = step == ahead - 1
        up, down = on_chip(
            functools.partial(ring_kernel, step),
            "ring_step",
            [((rows, width), bf16), ((rows, width), f32 if last else bf16)],
            (info, own, crossed[step], *arrived),
        )
        up = along_z(up, 1)
        if not last:
            down = along_z(down, -1)
    done = (down + up.astype(f32)).astype(bf16)

    ups, downs = [done], [done]
    pieces = []

    def spread(blocks, offsets):
        stack = jnp.stack(blocks) if len(blocks) > 1 else blocks[0]
        index = range(len(blocks)) if len(blocks) > 1 else [None]
        crossed = to_x(stack)
        for array, core_flip, side_flip in (
            (stack, False, False),
            (crossed, False, True),
            (to_core(stack), True, False),
            (to_core(crossed), True, True),
        ):
            for i, offset in zip(index, offsets):
                pieces.append((array, i, offset, core_flip, side_flip))

    for step in range(1, ahead + 1):
        ups.append(along_z(ups[-1], 1))
        if step <= behind:
            downs.append(along_z(downs[-1], -1))
        if step == 1:
            spread([done, ups[1], downs[1]], [0, -1, 1])
        elif step <= behind:
            spread([ups[step], downs[step]], [-step, step])
            if step == behind - 1:
                early = place_call(info, pieces, (width, width), ring, None)
                pieces.clear()
        else:
            spread([ups[step]], [-step])
    whole, edge = place_call(info, pieces, (width, width), ring, early)
    edge = edge[:, 0]
    return whole, edge[:TAPS], edge[TAPS:]


def body(mels, lengths, sub_weight, block_weight, conv_kernel, norm_gain, cotangent):
    weight = block_weight[0]
    taps = conv_kernel[0]
    gain = norm_gain
    width = cotangent.shape[1]
    groups = lengths.shape[0]
    sections = lax.axis_size("section")
    shards = lax.axis_size("dp")
    section_idx = lax.axis_index("section")
    crossing = sections // 2

    def flip(shard):
        return (shard + shards // 2) % shards

    def linear(shard, section):
        return shard * sections + section

    def relay(block, pairs):
        route = []
        for source, target in pairs:
            crossed = (source < crossing) != (target < crossing)
            for shard in range(shards):
                there = flip(shard) if crossed else shard
                route.append((linear(shard, source), linear(there, target)))
        return lax.ppermute(block, ("dp", "section"), route)

    upper = range(crossing, sections)
    lens_flipped = lax.ppermute(
        lengths,
        ("dp", "section"),
        [(linear(d, s), linear(flip(d), s)) for d in range(shards) for s in upper],
    )
    lens = jnp.where(section_idx >= crossing, lens_flipped, lengths)
    seeds = lax.ppermute(
        cotangent,
        ("dp", "section"),
        [(linear(d, sections - 1), linear(flip(d), sections - 1)) for d in range(shards)],
    ).reshape(groups, FRAMES, width)
    subs = (
        jnp.dot(
            mels.reshape(groups * FRAMES, -1), sub_weight, preferred_element_type=jnp.float32
        )
        .astype(jnp.bfloat16)
        .reshape(groups, FRAMES, width)
    )
    shard = lax.axis_index("dp")
    spot = jnp.stack([shard % 2, (shard // 2) % (shards // 4), shard // (shards // 2)])
    info = jnp.concatenate([section_idx.reshape(1), lens, spot]).astype(jnp.int32)
    turn = sections - 1
    ticks = turn + groups
    stash = held = sums = None
    fwd_recv = {}
    bwd_recv = {}
    idle = jnp.zeros((FRAMES, width), jnp.bfloat16)
    for tick in range(turn + ticks):
        if tick < ticks:
            block, stash = forward_call(
                tick, info, fwd_recv.pop(tick - 1, idle), subs, weight, taps, gain, stash
            )
            pairs = [(s, s + 1) for s in range(sections - 1) if 0 <= tick - s < groups]
            if pairs:
                fwd_recv[tick] = relay(block, pairs)
        back = tick - turn
        if back >= 0:
            block, held = backward_call(
                back, sections, info, bwd_recv.pop(back - 1, idle), seeds, weight, taps, gain, stash, held
            )
            pairs = [
                (s, s - 1)
                for s in range(1, sections)
                if 0 <= back - (sections - 1 - s) < groups
            ]
            if pairs:
                bwd_recv[back] = relay(block, pairs)
            sums = taps_call(back, sections, info, held, stash, gain, sums)
    weight_sum, taps_sums, gain_sum = column_sum(info, stash[3], held[0], sums, shards)
    return (weight_sum[None], taps_sums[None], gain_sum)


def solution(mesh):
    return jax.shard_map(
        body,
        mesh=mesh,
        in_specs=(
            P("dp", None),
            P("dp"),
            P(),
            P("section", None, None),
            P("section", None, None),
            P("section", None),
            P("dp", None),
        ),
        out_specs=(P("section", None, None), P("section", None, None), P("section", None)),
        check_vma=False,
    )
```

```python
import functools
import jax
import jax.numpy as jnp
from jax import lax
from jax.experimental import pallas as pl
from jax.experimental.pallas import tpu as pltpu
from jax.sharding import PartitionSpec as P

FRAMES = 96
EPS = 1e-05
LANES = 128
PAD = 16
TAPS = 31
BLOCK = 256
VMEM = 16 * 2**20


def taps_sum(padded, taps, cols, reverse):
    total = None
    for low in range(8):
        shifted = padded[pl.ds(low, FRAMES + 24), :]
        for high in range(4):
            j = 8 * high + low - 1
            if 0 <= j < TAPS:
                row = TAPS - 1 - j if reverse else j
                term = taps[0, row : row + 1, cols] * shifted[8 * high : 8 * high + FRAMES]
                total = term if total is None else total + term
    return total


def lane_tile(tile):
    return pl.ds(pl.multiple_of(tile * LANES, LANES), LANES)


def lane_block(chunk):
    return pl.ds(pl.multiple_of(chunk * BLOCK, BLOCK), BLOCK)


def clear_rims(padded):
    rim = jnp.zeros((padded.shape[0], PAD, LANES), jnp.float32)
    padded[:, 0:PAD, :] = rim
    padded[:, PAD + FRAMES :, :] = rim


def frame_rows(length):
    rows = lax.broadcasted_iota(jnp.int32, (FRAMES, LANES), 0)
    return (rows < length).astype(jnp.float32)


def forward_kernel(tick, sections, info, recv, subs, weight, taps, gain, *rest):
    out, conv_all, norm_all, inv_all, hid_all, block_in, padded, total = rest[-8:]
    section = info[0]
    slot = tick - section
    width = out.shape[1]
    tiles = width // LANES
    chunks = width // BLOCK
    zeros = jnp.zeros((FRAMES, LANES), jnp.float32)

    @pl.when((slot >= 0) & (slot < subs.shape[0]))
    def _():
        @pl.when(section == 0)
        def _():
            block_in[...] = subs[slot]

        @pl.when(section != 0)
        def _():
            block_in[...] = recv[...]

        clear_rims(padded)
        mask = frame_rows(info[1 + slot])

        def add_up(tile, sums):
            return sums + block_in[:, lane_tile(tile)].astype(jnp.float32)

        centre = jnp.sum(lax.fori_loop(0, tiles, add_up, zeros, unroll=4), axis=1, keepdims=True)
        centre = jnp.broadcast_to(centre * (1.0 / width), (FRAMES, LANES))

        def add_squares(tile, sums):
            gap = block_in[:, lane_tile(tile)].astype(jnp.float32) - centre
            return sums + gap * gap

        spread = jnp.sum(
            lax.fori_loop(0, tiles, add_squares, zeros, unroll=4), axis=1, keepdims=True
        )
        inv_std = jnp.broadcast_to(lax.rsqrt(spread * (1.0 / width) + EPS), (FRAMES, LANES))
        inv_all[slot] = inv_std
        total[...] = block_in[...].astype(jnp.float32)
        hid_all[slot, :, 0:BLOCK] = jnp.zeros((FRAMES, BLOCK), jnp.bfloat16)

        def project(chunk):
            cols = lane_block(chunk)
            total[...] += jnp.dot(
                hid_all[slot, :, cols], weight[cols, :], preferred_element_type=jnp.float32
            )

        def one_chunk(chunk):
            for step in range(BLOCK // LANES):
                cols = lane_tile(chunk * (BLOCK // LANES) + step)
                normed = (block_in[:, cols].astype(jnp.float32) - centre) * inv_std
                norm_all[slot, :, cols] = normed
                padded[step, PAD : PAD + FRAMES, :] = normed * gain[:, cols] * mask
                conv = taps_sum(padded.at[step], taps, cols, False)
                conv_all[slot, :, cols] = conv
                hid_all[slot, :, cols] = (conv / (1.0 + jnp.exp(-conv))).astype(jnp.bfloat16)

        @pl.when(section != sections - 1)
        def _():
            def with_project(chunk, carry):
                project(jnp.maximum(chunk - 1, 0))
                one_chunk(chunk)
                return carry

            lax.fori_loop(0, chunks, with_project, 0)
            project(chunks - 1)
            out[...] = total[...].astype(jnp.bfloat16)

        @pl.when(section == sections - 1)
        def _():
            def without(chunk, carry):
                one_chunk(chunk)
                return carry

            lax.fori_loop(0, chunks, without, 0)


def forward_call(tick, sections, info, recv, subs, weight, taps, gain, stash):
    groups, _, width = subs.shape
    f32, bf16 = jnp.float32, jnp.bfloat16
    shapes = (
        jax.ShapeDtypeStruct((FRAMES, width), bf16),
        jax.ShapeDtypeStruct((groups, FRAMES, width), f32),
        jax.ShapeDtypeStruct((groups, FRAMES, width), f32),
        jax.ShapeDtypeStruct((groups, FRAMES, LANES), f32),
        jax.ShapeDtypeStruct((groups, FRAMES, width), bf16),
    )
    smem = pl.BlockSpec(memory_space=pltpu.SMEM)
    vmem = pl.BlockSpec(memory_space=pltpu.VMEM)
    held = () if stash is None else tuple(stash)
    res = pl.pallas_call(
        functools.partial(forward_kernel, tick, sections),
        out_shape=shapes,
        in_specs=[smem] + [vmem] * (5 + len(held)),
        out_specs=(vmem,) * 5,
        scratch_shapes=[
            pltpu.VMEM((FRAMES, width), bf16),
            pltpu.VMEM((BLOCK // LANES, FRAMES + 2 * PAD, LANES), f32),
            pltpu.VMEM((FRAMES, width), f32),
        ],
        input_output_aliases={6 + i: 1 + i for i in range(len(held))},
        compiler_params=pltpu.CompilerParams(vmem_limit_bytes=VMEM),
        cost_estimate=pl.CostEstimate(
            flops=10**6, bytes_accessed=2**10, transcendentals=0
        ),
        name="section_forward",
    )(info, recv, subs, weight, taps, gain, *held)
    return res[0], res[1:]


def backward_kernel(tick, sections, info, seeds, recv, crossed, weight, taps, gain, conv_all, norm_all, inv_all, *rest):
    out, grad_all, gconv_all, gain_all = rest[-10:-6]
    grad_out, padded, scaled_now, ahead, mean_sum, dot_sum = rest[-6:]
    section = info[0]
    late = jnp.where(section < sections // 2, 1, 0)
    slot = tick - (sections - 1 - section) - late
    width = out.shape[1]
    tiles = width // LANES
    chunks = width // BLOCK

    groups = grad_all.shape[0]

    @pl.when((slot >= 0) & (slot < groups))
    def _():
        mask = frame_rows(info[1 + slot])

        @pl.when(section == sections - 1)
        def _():
            def seed(tile, carry):
                cols = lane_tile(tile)
                masked = seeds[slot, :, cols].astype(jnp.float32) * mask
                grad_out[:, cols] = masked.astype(jnp.bfloat16)
                return carry

            lax.fori_loop(0, tiles, seed, 0)

        @pl.when(section == sections // 2 - 1)
        def _():
            grad_out[...] = crossed[...]

        @pl.when((section != sections - 1) & (section != sections // 2 - 1))
        def _():
            grad_out[...] = recv[...]

        clear_rims(padded)
        grad_all[slot] = grad_out[...]
        mean_sum[...] = jnp.zeros((FRAMES, LANES), jnp.float32)
        dot_sum[...] = jnp.zeros((FRAMES, LANES), jnp.float32)

        def back_project(chunk):
            return lax.dot_general(
                grad_out[...],
                weight[lane_block(chunk), :],
                (((1,), (1,)), ((), ())),
                preferred_element_type=jnp.float32,
            )

        ahead[0] = back_project(0)

        def one_chunk(chunk, carry):
            grad_hidden = ahead[chunk % 2]
            ahead[(chunk + 1) % 2] = back_project(jnp.minimum(chunk + 1, chunks - 1))
            for step in range(BLOCK // LANES):
                cols = lane_tile(chunk * (BLOCK // LANES) + step)
                conv = conv_all[slot, :, cols]
                sigma = 1.0 / (1.0 + jnp.exp(-conv))
                gconv = grad_hidden[:, step * LANES : (step + 1) * LANES] * sigma * (
                    1.0 + conv * (1.0 - sigma)
                )
                gconv_all[slot, :, cols] = gconv
                padded[step, PAD : PAD + FRAMES, :] = gconv
                grad_normed = taps_sum(padded.at[step], taps, cols, True) * mask
                normed = norm_all[slot, :, cols]
                product = grad_normed * normed
                part = product[0:8]
                for row in range(8, FRAMES, 8):
                    part = part + product[row : row + 8]
                gain_all[slot, :, cols] = part
                scaled = grad_normed * gain[:, cols]
                scaled_now[:, cols] = scaled
                mean_sum[...] += scaled
                dot_sum[...] += scaled * normed
            return carry

        lax.fori_loop(0, chunks, one_chunk, 0)
        mean_row = jnp.sum(mean_sum[...], axis=1, keepdims=True) * (1.0 / width)
        dot_row = jnp.sum(dot_sum[...], axis=1, keepdims=True) * (1.0 / width)
        mean_row = jnp.broadcast_to(mean_row, (FRAMES, LANES))
        dot_row = jnp.broadcast_to(dot_row, (FRAMES, LANES))
        inv_std = inv_all[slot]

        def finish(tile, carry):
            cols = lane_tile(tile)
            change = inv_std * (scaled_now[:, cols] - mean_row - norm_all[slot, :, cols] * dot_row)
            out[:, cols] = (grad_out[:, cols].astype(jnp.float32) + change).astype(jnp.bfloat16)
            return carry

        lax.fori_loop(0, tiles, finish, 0, unroll=2)


def backward_call(tick, sections, info, seeds, recv, crossed, weight, taps, gain, stash, held):
    groups, _, width = stash[0].shape
    f32, bf16 = jnp.float32, jnp.bfloat16
    shapes = (
        jax.ShapeDtypeStruct((FRAMES, width), bf16),
        jax.ShapeDtypeStruct((groups, FRAMES, width), bf16),
        jax.ShapeDtypeStruct((groups, FRAMES, width), f32),
        jax.ShapeDtypeStruct((groups, 8, width), f32),
    )
    smem = pl.BlockSpec(memory_space=pltpu.SMEM)
    vmem = pl.BlockSpec(memory_space=pltpu.VMEM)
    held = () if held is None else tuple(held)
    res = pl.pallas_call(
        functools.partial(backward_kernel, tick, sections),
        out_shape=shapes,
        in_specs=[smem] + [vmem] * (9 + len(held)),
        out_specs=(vmem,) * 4,
        scratch_shapes=[
            pltpu.VMEM((FRAMES, width), bf16),
            pltpu.VMEM((BLOCK // LANES, FRAMES + 2 * PAD, LANES), f32),
            pltpu.VMEM((FRAMES, width), f32),
            pltpu.VMEM((2, FRAMES, BLOCK), f32),
            pltpu.VMEM((FRAMES, LANES), f32),
            pltpu.VMEM((FRAMES, LANES), f32),
        ],
        input_output_aliases={10 + i: 1 + i for i in range(len(held))},
        compiler_params=pltpu.CompilerParams(vmem_limit_bytes=VMEM),
        cost_estimate=pl.CostEstimate(
            flops=10**6, bytes_accessed=2**10, transcendentals=0
        ),
        name="section_backward",
    )(info, seeds, recv, crossed, weight, taps, gain, *stash[:3], *held)
    return res[0], res[1:]


def taps_kernel(tick, sections, info, gconv_all, norm_all, gain, gain_all, *rest):
    out, padded = rest[-2:]
    groups = gconv_all.shape[0]
    late = jnp.where(info[0] >= sections // 2, groups, 1)
    slot = tick - (sections - 1 - info[0]) - late
    width = out.shape[1]
    if len(rest) == 2:
        out[...] = jnp.zeros(out.shape, jnp.float32)

    @pl.when((slot >= 0) & (slot < gconv_all.shape[0]))
    def _():
        mask = frame_rows(info[1 + slot])
        clear_rims(padded)

        def one_tile(tile, carry):
            cols = lane_tile(tile)
            padded[0, PAD : PAD + FRAMES, :] = norm_all[slot, :, cols] * gain[:, cols] * mask
            grads = gconv_all[slot, :, cols]
            for low in range(8):
                shifted = padded[0, pl.ds(low, FRAMES + 24), :]
                for high in range(4):
                    j = 8 * high + low - 1
                    if 0 <= j < TAPS:
                        product = grads * shifted[8 * high : 8 * high + FRAMES]
                        part = product[0:8]
                        for row in range(8, FRAMES, 8):
                            part = part + product[row : row + 8]
                        out[j : j + 1, cols] += jnp.sum(part, axis=0, keepdims=True)
            out[TAPS : TAPS + 1, cols] += jnp.sum(gain_all[slot, :, cols], axis=0, keepdims=True)
            return carry

        lax.fori_loop(0, width // LANES, one_tile, 0)


def on_chip(kernel, name, shapes, operands, scratch=(), aliases=None, hbm_out=()):
    vmem = pl.BlockSpec(memory_space=pltpu.VMEM)
    smem = pl.BlockSpec(memory_space=pltpu.SMEM)
    anywhere = pl.BlockSpec(memory_space=pl.ANY)
    aliases = aliases or {}
    return pl.pallas_call(
        kernel,
        out_shape=tuple(jax.ShapeDtypeStruct(shape, dtype) for shape, dtype in shapes),
        in_specs=[smem]
        + [anywhere if aliases.get(i + 1) in hbm_out else vmem for i in range(len(operands) - 1)],
        out_specs=tuple(anywhere if i in hbm_out else vmem for i in range(len(shapes))),
        scratch_shapes=list(scratch),
        input_output_aliases=aliases,
        compiler_params=pltpu.CompilerParams(vmem_limit_bytes=VMEM),
        cost_estimate=pl.CostEstimate(flops=10**6, bytes_accessed=2**10, transcendentals=0),
        name=name,
    )(*operands)


def taps_call(tick, sections, info, held, stash, gain, sums):
    width = gain.shape[1]
    operands = (info, held[1], stash[1], gain, held[2]) + (() if sums is None else (sums,))
    return on_chip(
        functools.partial(taps_kernel, tick, sections),
        "taps_gradient",
        [((TAPS + 1, width), jnp.float32)],
        operands,
        [pltpu.VMEM((1, FRAMES + 2 * PAD, LANES), jnp.float32)],
        {} if sums is None else {5: 0},
    )[0]


EXTRA = 8


def part_kernel(own, info, hid_all, grad_all, out):
    ring, sides, cut, width = out.shape
    half = info[5] if own else 1 - info[5]
    piece = 8 * cut
    tokens = hid_all.shape[0] * FRAMES
    grads = grad_all[...].reshape(tokens, width)
    for step in range(ring * sides * cut // piece):
        start = pl.multiple_of(half * (ring * sides * cut) + step * piece, LANES)
        hidden = hid_all[:, :, pl.ds(start, piece)].reshape(tokens, piece)
        part = lax.dot_general(
            hidden, grads, (((0,), (0,)), ((), ())), preferred_element_type=jnp.float32
        )
        for i in range(piece // cut):
            block = step * (piece // cut) + i
            out[block // sides, block % sides] = part[i * cut : (i + 1) * cut].astype(jnp.bfloat16)


def ring_kernel(step, info, mine, other, sums, sums_other, *rest):
    ring, sides, cut, width = mine.shape
    core, place, side = info[5], info[6], info[7]
    ahead, behind = ring // 2, ring - 1 - ring // 2
    f32 = jnp.float32
    blank = jnp.zeros((EXTRA - 1, width), f32)

    def fill(target, owner, x, *more):
        owner = owner % ring
        total = mine[owner, x].astype(f32) + other[owner, x].astype(f32)
        index = pl.ds((core * ring + owner) * sides + x, 1)
        edge = jnp.concatenate([sums[index, :] + sums_other[index, :], blank], axis=0)
        for block in more:
            total = total + block[:cut].astype(f32)
            edge = edge + block[cut:].astype(f32)
        target[:cut] = total.astype(target.dtype)
        target[cut:] = edge.astype(target.dtype)

    if step < 0:
        for i in range(ahead):
            fill(rest[i].at[0], place + ahead - i, 1 - side)
            fill(rest[i].at[1], place + ring - behind + i, 1 - side)
        return
    crossed, arrived = rest[0], rest[1:-2]
    up, down = rest[-2:]
    fill(up, place + ahead - step, side, crossed[0], *arrived[:1])
    fill(down, place + ring - behind + step, side, crossed[1], *arrived[1:])


def place_kernel(ring, sources, count, last, info, *rest):
    blocks = rest[:count]
    whole, edge = rest[-5:-3] if last else rest[-3:-1]
    sems = rest[-1]
    core, place, side = info[5], info[6], info[7]
    cut = blocks[0].shape[-2] - EXTRA
    copies = []
    for n, (which, i, offset, core_flip, side_flip) in enumerate(sources):
        block = blocks[which] if i is None else blocks[which].at[i]
        half = 1 - core if core_flip else core
        x = 1 - side if side_flip else side
        index = (half * ring + (place + offset + ring) % ring) * 2 + x
        start = pl.multiple_of(index * cut, cut)
        copy = pltpu.make_async_copy(
            block.at[pl.ds(0, cut)], whole.at[pl.ds(start, cut)], sems.at[n]
        )
        copy.start()
        copies.append(copy)
        edge[index] = block[cut:, :].astype(jnp.float32)
    if last:
        taps_out, gain_out = rest[-3:-1]
        for row in range(TAPS):
            taps_out[0, row : row + 1, :] = edge[row, 0:1, :]
        gain_out[...] = edge[TAPS, 0:1, :]
    for copy in copies:
        copy.wait()


def place_call(info, pieces, shape, ring, held):
    blocks, sources = [], []
    for block, i, offset, core_flip, side_flip in pieces:
        which = [n for n, other in enumerate(blocks) if other is block]
        if not which:
            which = [len(blocks)]
            blocks.append(block)
        sources.append((which[0], i, offset, core_flip, side_flip))
    count = len(blocks)
    return on_chip(
        functools.partial(place_kernel, ring, sources, count, held is not None),
        "place_sums",
        [(shape, jnp.bfloat16), ((4 * ring, EXTRA, shape[1]), jnp.float32)]
        + ([((1, TAPS, shape[1]), jnp.float32), ((1, shape[1]), jnp.float32)] if held else []),
        (info, *blocks, *(held or ())),
        [pltpu.SemaphoreType.DMA((len(sources),))],
        {count + 1: 0, count + 2: 1} if held else {},
        hbm_out=(0,),
    )


def column_sum(info, hidden, grads, sums, shards):
    ring = shards // 4
    width = grads.shape[2]
    cut = width // shards
    rows = cut + EXTRA
    f32, bf16 = jnp.float32, jnp.bfloat16

    def along_z(block, step):
        route = []
        for d in range(shards):
            x, z, c = d // (2 * ring), (d // 2) % ring, d % 2
            route.append((d, (x * ring + (z + step) % ring) * 2 + c))
        return lax.ppermute(block, "dp", route)

    def to_core(block):
        return lax.ppermute(block, "dp", [(d, d ^ 1) for d in range(shards)])

    def to_x(block):
        return lax.ppermute(block, "dp", [(d, (d + shards // 2) % shards) for d in range(shards)])

    def part(own):
        return on_chip(
            functools.partial(part_kernel, own),
            "weight_part",
            [((ring, 2, cut, width), bf16)],
            (info, hidden, grads),
        )[0]

    other = to_core(part(False))
    sums = sums()
    sums_other = to_core(sums)
    mine = part(True)
    ahead, behind = ring // 2, ring - 1 - ring // 2
    block, pair = ((rows, width), bf16), ((2, rows, width), bf16)

    def ring_call(step, *arrived):
        shapes = [block, ((rows, width), f32) if step == ahead - 1 else block]
        return on_chip(
            functools.partial(ring_kernel, step),
            "ring_step",
            shapes if step >= 0 else [pair] * ahead,
            (info, mine, other, sums, sums_other, *arrived),
        )

    crossed = [to_x(send) for send in ring_call(-1)]
    arrived = ()
    for step in range(ahead):
        up, down = ring_call(step, crossed[step], *arrived)
        up = along_z(up, 1)
        if step < ahead - 1:
            down = along_z(down, -1)
        arrived = (up, down)
    done = (down + up.astype(f32)).astype(bf16)

    ups, downs = [done], [done]
    stacks, swaps, tags = [], [], []
    for step in range(1, ahead + 1):
        ups.append(along_z(ups[-1], 1))
        if step <= behind:
            downs.append(along_z(downs[-1], -1))
        if step > 1:
            swaps.append(to_x(stacks[-1]))
        fresh = [(-step, ups[step])] + ([(step, downs[step])] if step <= behind else [])
        if step == 1:
            fresh = [(0, done)] + fresh
        tags.append([offset for offset, _ in fresh])
        stacks.append(jnp.stack([piece for _, piece in fresh]))
    swaps.append(to_x(stacks[-1]))

    def batch(groups):
        joined = jnp.concatenate([stack for stack, _, _ in groups])
        turned = to_core(joined)
        pieces = []
        count = 0
        for stack, offsets, side_flip in groups:
            for i, offset in enumerate(offsets):
                pieces.append((stack, i, offset, False, side_flip))
                pieces.append((turned, count, offset, True, side_flip))
                count += 1
        return pieces

    early = [(stacks[i], tags[i], False) for i in range(behind)]
    early += [(swaps[i], tags[i], True) for i in range(behind - 1)]
    middle = [(stacks[behind], tags[behind], False), (swaps[behind - 1], tags[behind - 1], True)]
    late = [(swaps[behind], tags[behind], True)]
    held = place_call(info, batch(early), (width, width), ring, None)
    whole, _, taps_sums, gain_sum = place_call(
        info, batch(middle + late), (width, width), ring, held
    )
    return whole, taps_sums, gain_sum


def body(mels, lengths, sub_weight, block_weight, conv_kernel, norm_gain, cotangent):
    weight = block_weight[0]
    taps = conv_kernel
    gain = norm_gain
    width = cotangent.shape[1]
    groups = lengths.shape[0]
    sections = lax.axis_size("section")
    shards = lax.axis_size("dp")
    section_idx = lax.axis_index("section")
    crossing = sections // 2

    def flip(shard):
        return (shard + shards // 2) % shards

    def linear(shard, section):
        return shard * sections + section

    def relay(block, pairs):
        route = []
        for source, target in pairs:
            crossed = (source < crossing) != (target < crossing)
            for shard in range(shards):
                there = flip(shard) if crossed else shard
                route.append((linear(shard, source), linear(there, target)))
        return lax.ppermute(block, ("dp", "section"), route)

    upper = range(crossing, sections)
    lens_flipped = lax.ppermute(
        lengths,
        ("dp", "section"),
        [(linear(d, s), linear(flip(d), s)) for d in range(shards) for s in upper],
    )
    lens = jnp.where(section_idx >= crossing, lens_flipped, lengths)
    seeds = lax.ppermute(
        cotangent,
        ("dp", "section"),
        [(linear(d, sections - 1), linear(flip(d), sections - 1)) for d in range(shards)],
    ).reshape(groups, FRAMES, width)
    subs = (
        jnp.dot(
            mels.reshape(groups * FRAMES, -1), sub_weight, preferred_element_type=jnp.float32
        )
        .astype(jnp.bfloat16)
        .reshape(groups, FRAMES, width)
    )
    shard = lax.axis_index("dp")
    spot = jnp.stack([shard % 2, (shard // 2) % (shards // 4), shard // (shards // 2)])
    info = jnp.concatenate([section_idx.reshape(1), lens, spot]).astype(jnp.int32)
    turn = sections - 1
    ticks = turn + groups
    stash = held = sums = None
    idle = jnp.zeros((FRAMES, width), jnp.bfloat16)
    forward_recv = backward_recv = idle

    half = sections // 2
    crossed = {}
    for tick in range(turn + ticks + 1):
        back = tick - turn
        if tick < ticks:
            block, stash = forward_call(
                tick, sections, info, forward_recv, subs, weight, taps, gain, stash
            )
            pairs = [(s, s + 1) for s in range(sections - 1) if 0 <= tick - s < groups]
            forward_recv = relay(block, pairs) if pairs else idle
        if back < 0:
            continue
        block, held = backward_call(
            back, sections, info, seeds, backward_recv, crossed.get(back - 2, idle),
            weight, taps, gain, stash, held,
        )
        active = [
            s
            for s in range(1, sections)
            if 0 <= back - (sections - 1 - s) - (1 if s < half else 0) < groups
        ]
        pairs = [(s, s - 1) for s in active if s != half]
        backward_recv = relay(block, pairs) if pairs else idle
        if half in active:
            crossed[back] = relay(block, [(half, half - 1)])
        if groups <= back < ticks:
            sums = taps_call(back, sections, info, held, stash, gain, sums)

    def last_sums():
        return taps_call(ticks, sections, info, held, stash, gain, sums)

    weight_sum, taps_sums, gain_sum = column_sum(info, stash[3], held[0], last_sums, shards)
    return (weight_sum[None], taps_sums, gain_sum)


def solution(mesh):
    return jax.shard_map(
        body,
        mesh=mesh,
        in_specs=(
            P("dp", None),
            P("dp"),
            P(),
            P("section", None, None),
            P("section", None, None),
            P("section", None),
            P("dp", None),
        ),
        out_specs=(P("section", None, None), P("section", None, None), P("section", None)),
        check_vma=False,
    )
```

```python
import functools
import jax
import jax.numpy as jnp
from jax import lax
from jax.experimental import pallas as pl
from jax.experimental.pallas import tpu as pltpu
from jax.sharding import PartitionSpec as P

FRAMES = 96
EPS = 1e-05
LANES = 128
PAD = 16
TAPS = 31
BLOCK = 256
VMEM = 16 * 2**20


def taps_sum(padded, taps, cols, reverse):
    total = None
    for low in range(8):
        shifted = padded[pl.ds(low, FRAMES + 24), :]
        for high in range(4):
            j = 8 * high + low - 1
            if 0 <= j < TAPS:
                row = TAPS - 1 - j if reverse else j
                term = taps[row, :, cols] * shifted[8 * high : 8 * high + FRAMES]
                total = term if total is None else total + term
    return total


def lane_tile(tile):
    return pl.ds(pl.multiple_of(tile * LANES, LANES), LANES)


def lane_block(chunk):
    return pl.ds(pl.multiple_of(chunk * BLOCK, BLOCK), BLOCK)


def clear_rims(padded):
    rim = jnp.zeros((padded.shape[0], PAD, LANES), jnp.float32)
    padded[:, 0:PAD, :] = rim
    padded[:, PAD + FRAMES :, :] = rim


def frame_rows(length):
    rows = lax.broadcasted_iota(jnp.int32, (FRAMES, LANES), 0)
    return (rows < length).astype(jnp.float32)


def forward_kernel(tick, sections, info, recv, subs, weight, taps, gain, *rest):
    out, conv_all, norm_all, inv_all, hid_all, block_in, padded, total = rest[-8:]
    section = info[0]
    slot = tick - section
    width = out.shape[1]
    tiles = width // LANES
    chunks = width // BLOCK
    zeros = jnp.zeros((FRAMES, LANES), jnp.float32)

    @pl.when((slot >= 0) & (slot < subs.shape[0]))
    def _():
        @pl.when(section == 0)
        def _():
            block_in[...] = subs[slot]

        @pl.when(section != 0)
        def _():
            block_in[...] = recv[...]

        clear_rims(padded)
        mask = frame_rows(info[1 + slot])

        def add_up(tile, sums):
            return sums + block_in[:, lane_tile(tile)].astype(jnp.float32)

        centre = jnp.sum(lax.fori_loop(0, tiles, add_up, zeros, unroll=4), axis=1, keepdims=True)
        centre = jnp.broadcast_to(centre * (1.0 / width), (FRAMES, LANES))

        def add_squares(tile, sums):
            gap = block_in[:, lane_tile(tile)].astype(jnp.float32) - centre
            return sums + gap * gap

        spread = jnp.sum(
            lax.fori_loop(0, tiles, add_squares, zeros, unroll=4), axis=1, keepdims=True
        )
        inv_std = jnp.broadcast_to(lax.rsqrt(spread * (1.0 / width) + EPS), (FRAMES, LANES))
        inv_all[slot] = inv_std
        total[...] = block_in[...].astype(jnp.float32)
        hid_all[slot, :, 0:BLOCK] = jnp.zeros((FRAMES, BLOCK), jnp.bfloat16)

        def project(chunk):
            cols = lane_block(chunk)
            total[...] += jnp.dot(
                hid_all[slot, :, cols], weight[cols, :], preferred_element_type=jnp.float32
            )

        def one_chunk(chunk):
            for step in range(BLOCK // LANES):
                cols = lane_tile(chunk * (BLOCK // LANES) + step)
                normed = (block_in[:, cols].astype(jnp.float32) - centre) * inv_std
                norm_all[slot, :, cols] = normed
                padded[step, PAD : PAD + FRAMES, :] = normed * gain[:, cols] * mask
                conv = taps_sum(padded.at[step], taps, cols, False)
                conv_all[slot, :, cols] = conv
                hid_all[slot, :, cols] = (conv / (1.0 + jnp.exp(-conv))).astype(jnp.bfloat16)

        @pl.when(section != sections - 1)
        def _():
            def with_project(chunk, carry):
                project(jnp.maximum(chunk - 1, 0))
                one_chunk(chunk)
                return carry

            lax.fori_loop(0, chunks, with_project, 0)
            project(chunks - 1)
            out[...] = total[...].astype(jnp.bfloat16)

        @pl.when(section == sections - 1)
        def _():
            def without(chunk, carry):
                one_chunk(chunk)
                return carry

            lax.fori_loop(0, chunks, without, 0)


def forward_call(tick, sections, info, recv, subs, weight, taps, gain, stash):
    groups, _, width = subs.shape
    f32, bf16 = jnp.float32, jnp.bfloat16
    shapes = (
        jax.ShapeDtypeStruct((FRAMES, width), bf16),
        jax.ShapeDtypeStruct((groups, FRAMES, width), f32),
        jax.ShapeDtypeStruct((groups, FRAMES, width), f32),
        jax.ShapeDtypeStruct((groups, FRAMES, LANES), f32),
        jax.ShapeDtypeStruct((groups, FRAMES, width), bf16),
    )
    smem = pl.BlockSpec(memory_space=pltpu.SMEM)
    vmem = pl.BlockSpec(memory_space=pltpu.VMEM)
    held = () if stash is None else tuple(stash)
    res = pl.pallas_call(
        functools.partial(forward_kernel, tick, sections),
        out_shape=shapes,
        in_specs=[smem] + [vmem] * (5 + len(held)),
        out_specs=(vmem,) * 5,
        scratch_shapes=[
            pltpu.VMEM((FRAMES, width), bf16),
            pltpu.VMEM((BLOCK // LANES, FRAMES + 2 * PAD, LANES), f32),
            pltpu.VMEM((FRAMES, width), f32),
        ],
        input_output_aliases={6 + i: 1 + i for i in range(len(held))},
        compiler_params=pltpu.CompilerParams(vmem_limit_bytes=VMEM),
        cost_estimate=pl.CostEstimate(
            flops=10**6, bytes_accessed=2**10, transcendentals=0
        ),
        name="section_forward",
    )(info, recv, subs, weight, taps, gain, *held)
    return res[0], res[1:]


def backward_kernel(tick, sections, info, seeds, recv, crossed, weight, taps, gain, conv_all, norm_all, inv_all, *rest):
    out, grad_all, gconv_all, gain_all = rest[-10:-6]
    grad_out, padded, scaled_now, ahead, mean_sum, dot_sum = rest[-6:]
    section = info[0]
    late = jnp.where(section < sections // 2, 1, 0)
    slot = tick - (sections - 1 - section) - late
    width = out.shape[1]
    tiles = width // LANES
    chunks = width // BLOCK

    groups = grad_all.shape[0]

    @pl.when((slot >= 0) & (slot < groups))
    def _():
        mask = frame_rows(info[1 + slot])

        @pl.when(section == sections - 1)
        def _():
            def seed(tile, carry):
                cols = lane_tile(tile)
                masked = seeds[slot, :, cols].astype(jnp.float32) * mask
                grad_out[:, cols] = masked.astype(jnp.bfloat16)
                return carry

            lax.fori_loop(0, tiles, seed, 0)

        @pl.when(section == sections // 2 - 1)
        def _():
            grad_out[...] = crossed[...]

        @pl.when((section != sections - 1) & (section != sections // 2 - 1))
        def _():
            grad_out[...] = recv[...]

        clear_rims(padded)
        grad_all[slot] = grad_out[...]
        mean_sum[...] = jnp.zeros((FRAMES, LANES), jnp.float32)
        dot_sum[...] = jnp.zeros((FRAMES, LANES), jnp.float32)

        def back_project(chunk):
            return lax.dot_general(
                grad_out[...],
                weight[lane_block(chunk), :],
                (((1,), (1,)), ((), ())),
                preferred_element_type=jnp.float32,
            )

        ahead[0] = back_project(0)

        def one_chunk(chunk, carry):
            grad_hidden = ahead[chunk % 2]
            ahead[(chunk + 1) % 2] = back_project(jnp.minimum(chunk + 1, chunks - 1))
            for step in range(BLOCK // LANES):
                cols = lane_tile(chunk * (BLOCK // LANES) + step)
                conv = conv_all[slot, :, cols]
                sigma = 1.0 / (1.0 + jnp.exp(-conv))
                gconv = grad_hidden[:, step * LANES : (step + 1) * LANES] * sigma * (
                    1.0 + conv * (1.0 - sigma)
                )
                gconv_all[slot, :, cols] = gconv
                padded[step, PAD : PAD + FRAMES, :] = gconv
                grad_normed = taps_sum(padded.at[step], taps, cols, True) * mask
                normed = norm_all[slot, :, cols]
                product = grad_normed * normed
                part = product[0:8]
                for row in range(8, FRAMES, 8):
                    part = part + product[row : row + 8]
                gain_all[slot, :, cols] = part
                scaled = grad_normed * gain[:, cols]
                scaled_now[:, cols] = scaled
                mean_sum[...] += scaled
                dot_sum[...] += scaled * normed
            return carry

        lax.fori_loop(0, chunks, one_chunk, 0)

        @pl.when(section != 0)
        def _():
            mean_row = jnp.sum(mean_sum[...], axis=1, keepdims=True) * (1.0 / width)
            dot_row = jnp.sum(dot_sum[...], axis=1, keepdims=True) * (1.0 / width)
            mean_row = jnp.broadcast_to(mean_row, (FRAMES, LANES))
            dot_row = jnp.broadcast_to(dot_row, (FRAMES, LANES))
            inv_std = inv_all[slot]

            def finish(tile, carry):
                cols = lane_tile(tile)
                change = inv_std * (scaled_now[:, cols] - mean_row - norm_all[slot, :, cols] * dot_row)
                out[:, cols] = (grad_out[:, cols].astype(jnp.float32) + change).astype(jnp.bfloat16)
                return carry

            lax.fori_loop(0, tiles, finish, 0, unroll=2)


def backward_call(tick, sections, info, seeds, recv, crossed, weight, taps, gain, stash, held):
    groups, _, width = stash[0].shape
    f32, bf16 = jnp.float32, jnp.bfloat16
    shapes = (
        jax.ShapeDtypeStruct((FRAMES, width), bf16),
        jax.ShapeDtypeStruct((groups, FRAMES, width), bf16),
        jax.ShapeDtypeStruct((groups, FRAMES, width), f32),
        jax.ShapeDtypeStruct((groups, 8, width), f32),
    )
    smem = pl.BlockSpec(memory_space=pltpu.SMEM)
    vmem = pl.BlockSpec(memory_space=pltpu.VMEM)
    held = () if held is None else tuple(held)
    res = pl.pallas_call(
        functools.partial(backward_kernel, tick, sections),
        out_shape=shapes,
        in_specs=[smem] + [vmem] * (9 + len(held)),
        out_specs=(vmem,) * 4,
        scratch_shapes=[
            pltpu.VMEM((FRAMES, width), bf16),
            pltpu.VMEM((BLOCK // LANES, FRAMES + 2 * PAD, LANES), f32),
            pltpu.VMEM((FRAMES, width), f32),
            pltpu.VMEM((2, FRAMES, BLOCK), f32),
            pltpu.VMEM((FRAMES, LANES), f32),
            pltpu.VMEM((FRAMES, LANES), f32),
        ],
        input_output_aliases={10 + i: 1 + i for i in range(len(held))},
        compiler_params=pltpu.CompilerParams(vmem_limit_bytes=VMEM),
        cost_estimate=pl.CostEstimate(
            flops=10**6, bytes_accessed=2**10, transcendentals=0
        ),
        name="section_backward",
    )(info, seeds, recv, crossed, weight, taps, gain, *stash[:3], *held)
    return res[0], res[1:]


def taps_kernel(tick, sections, info, gconv_all, norm_all, gain, gain_all, *rest):
    out, padded = rest[-2:]
    groups = gconv_all.shape[0]
    late = jnp.where(info[0] >= sections // 2, groups, 1)
    slot = tick - (sections - 1 - info[0]) - late
    width = out.shape[1]
    if len(rest) == 2:
        out[...] = jnp.zeros(out.shape, jnp.float32)

    @pl.when((slot >= 0) & (slot < gconv_all.shape[0]))
    def _():
        mask = frame_rows(info[1 + slot])
        clear_rims(padded)

        def one_tile(tile, carry):
            cols = lane_tile(tile)
            padded[0, PAD : PAD + FRAMES, :] = norm_all[slot, :, cols] * gain[:, cols] * mask
            grads = gconv_all[slot, :, cols]
            for low in range(8):
                shifted = padded[0, pl.ds(low, FRAMES + 24), :]
                for high in range(4):
                    j = 8 * high + low - 1
                    if 0 <= j < TAPS:
                        product = grads * shifted[8 * high : 8 * high + FRAMES]
                        part = product[0:8]
                        for row in range(8, FRAMES, 8):
                            part = part + product[row : row + 8]
                        out[j : j + 1, cols] += jnp.sum(part, axis=0, keepdims=True)
            out[TAPS : TAPS + 1, cols] += jnp.sum(gain_all[slot, :, cols], axis=0, keepdims=True)
            return carry

        lax.fori_loop(0, width // LANES, one_tile, 0)


def on_chip(kernel, name, shapes, operands, scratch=(), aliases=None, hbm_out=(), flops=10**6):
    vmem = pl.BlockSpec(memory_space=pltpu.VMEM)
    smem = pl.BlockSpec(memory_space=pltpu.SMEM)
    anywhere = pl.BlockSpec(memory_space=pl.ANY)
    aliases = aliases or {}
    return pl.pallas_call(
        kernel,
        out_shape=tuple(jax.ShapeDtypeStruct(shape, dtype) for shape, dtype in shapes),
        in_specs=[smem]
        + [anywhere if aliases.get(i + 1) in hbm_out else vmem for i in range(len(operands) - 1)],
        out_specs=tuple(anywhere if i in hbm_out else vmem for i in range(len(shapes))),
        scratch_shapes=list(scratch),
        input_output_aliases=aliases,
        compiler_params=pltpu.CompilerParams(vmem_limit_bytes=VMEM),
        cost_estimate=pl.CostEstimate(flops=flops, bytes_accessed=2**10, transcendentals=0),
        name=name,
    )(*operands)


def taps_call(tick, sections, info, held, stash, gain, sums):
    width = gain.shape[1]
    operands = (info, held[1], stash[1], gain, held[2]) + (() if sums is None else (sums,))
    return on_chip(
        functools.partial(taps_kernel, tick, sections),
        "taps_gradient",
        [((TAPS + 1, width), jnp.float32)],
        operands,
        [pltpu.VMEM((1, FRAMES + 2 * PAD, LANES), jnp.float32)],
        {} if sums is None else {5: 0},
    )[0]


EXTRA = 8


def part_kernel(own, info, hid_all, grad_all, out):
    ring, sides, cut, width = out.shape
    half = info[5] if own else 1 - info[5]
    piece = 8 * cut
    tokens = hid_all.shape[0] * FRAMES
    grads = grad_all[...].reshape(tokens, width)
    for step in range(ring * sides * cut // piece):
        start = pl.multiple_of(half * (ring * sides * cut) + step * piece, LANES)
        hidden = hid_all[:, :, pl.ds(start, piece)].reshape(tokens, piece)
        part = lax.dot_general(
            hidden, grads, (((0,), (0,)), ((), ())), preferred_element_type=jnp.float32
        )
        for i in range(piece // cut):
            block = step * (piece // cut) + i
            out[block // sides, block % sides] = part[i * cut : (i + 1) * cut].astype(jnp.bfloat16)


def ring_kernel(step, info, mine, other, sums, sums_other, *rest):
    ring, sides, cut, width = mine.shape
    core, place, side = info[5], info[6], info[7]
    ahead, behind = ring // 2, ring - 1 - ring // 2
    f32 = jnp.float32
    blank = jnp.zeros((EXTRA - 1, width), f32)

    def fill(target, owner, x, *more):
        owner = owner % ring
        total = mine[owner, x].astype(f32) + other[owner, x].astype(f32)
        index = pl.ds((core * ring + owner) * sides + x, 1)
        edge = jnp.concatenate([sums[index, :] + sums_other[index, :], blank], axis=0)
        for block in more:
            total = total + block[:cut].astype(f32)
            edge = edge + block[cut:].astype(f32)
        target[:cut] = total.astype(target.dtype)
        target[cut:] = edge.astype(target.dtype)

    if step < 0:
        for i in range(ahead):
            fill(rest[i].at[0], place + ahead - i, 1 - side)
            fill(rest[i].at[1], place + ring - behind + i, 1 - side)
        return
    crossed, arrived = rest[0], rest[1:-2]
    up, down = rest[-2:]
    fill(up, place + ahead - step, side, crossed[0], *arrived[:1])
    fill(down, place + ring - behind + step, side, crossed[1], *arrived[1:])


def place_kernel(ring, sources, count, last, info, *rest):
    blocks = rest[:count]
    whole, edge = rest[-5:-3] if last else rest[-3:-1]
    sems = rest[-1]
    core, place, side = info[5], info[6], info[7]
    cut = blocks[0].shape[-2] - EXTRA
    copies = []
    for n, (which, i, offset, core_flip, side_flip) in enumerate(sources):
        block = blocks[which] if i is None else blocks[which].at[i]
        half = 1 - core if core_flip else core
        x = 1 - side if side_flip else side
        index = (half * ring + (place + offset + ring) % ring) * 2 + x
        start = pl.multiple_of(index * cut, cut)
        copy = pltpu.make_async_copy(
            block.at[pl.ds(0, cut)], whole.at[pl.ds(start, cut)], sems.at[n]
        )
        copy.start()
        copies.append(copy)
        edge[index] = block[cut:, :].astype(jnp.float32)
    if last:
        taps_out, gain_out = rest[-3:-1]
        for row in range(TAPS):
            taps_out[row] = edge[row, 0:1, :]
        gain_out[...] = edge[TAPS, 0:1, :]
    for copy in copies:
        copy.wait()


def place_call(info, pieces, shape, ring, held):
    blocks, sources = [], []
    for block, i, offset, core_flip, side_flip in pieces:
        which = [n for n, other in enumerate(blocks) if other is block]
        if not which:
            which = [len(blocks)]
            blocks.append(block)
        sources.append((which[0], i, offset, core_flip, side_flip))
    count = len(blocks)
    return on_chip(
        functools.partial(place_kernel, ring, sources, count, held is not None),
        "place_sums",
        [(shape, jnp.bfloat16), ((4 * ring, EXTRA, shape[1]), jnp.float32)]
        + ([((TAPS, 1, shape[1]), jnp.float32), ((1, shape[1]), jnp.float32)] if held else []),
        (info, *blocks, *(held or ())),
        [pltpu.SemaphoreType.DMA((len(sources),))],
        {count + 1: 0, count + 2: 1} if held else {},
        hbm_out=(0,),
        flops=10**6 if held else 5 * 10**9,
    )


def column_sum(info, hidden, grads, sums, shards):
    ring = shards // 4
    width = grads.shape[2]
    cut = width // shards
    rows = cut + EXTRA
    f32, bf16 = jnp.float32, jnp.bfloat16

    def along_z(block, step):
        route = []
        for d in range(shards):
            x, z, c = d // (2 * ring), (d // 2) % ring, d % 2
            route.append((d, (x * ring + (z + step) % ring) * 2 + c))
        return lax.ppermute(block, "dp", route)

    def to_core(block):
        return lax.ppermute(block, "dp", [(d, d ^ 1) for d in range(shards)])

    def to_x(block):
        return lax.ppermute(block, "dp", [(d, (d + shards // 2) % shards) for d in range(shards)])

    def part(own):
        return on_chip(
            functools.partial(part_kernel, own),
            "weight_part",
            [((ring, 2, cut, width), bf16)],
            (info, hidden, grads),
        )[0]

    other = to_core(part(False))
    sums = sums()
    sums_other = to_core(sums)
    mine = part(True)
    ahead, behind = ring // 2, ring - 1 - ring // 2
    block, pair = ((rows, width), bf16), ((2, rows, width), bf16)

    def ring_call(step, *arrived):
        shapes = [block, ((rows, width), f32) if step == ahead - 1 else block]
        return on_chip(
            functools.partial(ring_kernel, step),
            "ring_step",
            shapes if step >= 0 else [pair] * ahead,
            (info, mine, other, sums, sums_other, *arrived),
        )

    crossed = [to_x(send) for send in ring_call(-1)]
    arrived = ()
    for step in range(ahead):
        up, down = ring_call(step, crossed[step], *arrived)
        up = along_z(up, 1)
        if step < ahead - 1:
            down = along_z(down, -1)
        arrived = (up, down)
    done = (down + up.astype(f32)).astype(bf16)

    ups, downs = [done], [done]
    stacks, swaps, tags = [], [], []
    for step in range(1, ahead + 1):
        ups.append(along_z(ups[-1], 1))
        if step <= behind:
            downs.append(along_z(downs[-1], -1))
        if step > 1:
            swaps.append(to_x(stacks[-1]))
        fresh = [(-step, ups[step])] + ([(step, downs[step])] if step <= behind else [])
        if step == 1:
            fresh = [(0, done)] + fresh
        tags.append([offset for offset, _ in fresh])
        stacks.append(jnp.stack([piece for _, piece in fresh]))
    swaps.append(to_x(stacks[-1]))

    def batch(groups):
        joined = jnp.concatenate([stack for stack, _, _ in groups])
        turned = to_core(joined)
        pieces = []
        count = 0
        for stack, offsets, side_flip in groups:
            for i, offset in enumerate(offsets):
                pieces.append((stack, i, offset, False, side_flip))
                pieces.append((turned, count, offset, True, side_flip))
                count += 1
        return pieces

    early = [(stacks[i], tags[i], False) for i in range(behind)]
    early += [(swaps[i], tags[i], True) for i in range(behind - 1)]
    middle = [(stacks[behind], tags[behind], False), (swaps[behind - 1], tags[behind - 1], True)]
    late = [(swaps[behind], tags[behind], True)]
    held = place_call(info, batch(early), (width, width), ring, None)
    whole, _, taps_sums, gain_sum = place_call(
        info, batch(middle + late), (width, width), ring, held
    )
    return whole, taps_sums, gain_sum


def body(mels, lengths, sub_weight, block_weight, conv_kernel, norm_gain, cotangent):
    weight = block_weight[0]
    taps = jnp.transpose(conv_kernel, (1, 0, 2))
    gain = norm_gain
    width = cotangent.shape[1]
    groups = lengths.shape[0]
    sections = lax.axis_size("section")
    shards = lax.axis_size("dp")
    section_idx = lax.axis_index("section")
    crossing = sections // 2

    def flip(shard):
        return (shard + shards // 2) % shards

    def linear(shard, section):
        return shard * sections + section

    def relay(block, pairs):
        route = []
        for source, target in pairs:
            crossed = (source < crossing) != (target < crossing)
            for shard in range(shards):
                there = flip(shard) if crossed else shard
                route.append((linear(shard, source), linear(there, target)))
        return lax.ppermute(block, ("dp", "section"), route)

    upper = range(crossing, sections)
    lens_flipped = lax.ppermute(
        lengths,
        ("dp", "section"),
        [(linear(d, s), linear(flip(d), s)) for d in range(shards) for s in upper],
    )
    lens = jnp.where(section_idx >= crossing, lens_flipped, lengths)
    seeds = lax.ppermute(
        cotangent,
        ("dp", "section"),
        [(linear(d, sections - 1), linear(flip(d), sections - 1)) for d in range(shards)],
    ).reshape(groups, FRAMES, width)
    subs = (
        jnp.dot(
            mels.reshape(groups * FRAMES, -1), sub_weight, preferred_element_type=jnp.float32
        )
        .astype(jnp.bfloat16)
        .reshape(groups, FRAMES, width)
    )
    shard = lax.axis_index("dp")
    spot = jnp.stack([shard % 2, (shard // 2) % (shards // 4), shard // (shards // 2)])
    info = jnp.concatenate([section_idx.reshape(1), lens, spot]).astype(jnp.int32)
    turn = sections - 1
    ticks = turn + groups
    stash = held = sums = None
    idle = jnp.zeros((FRAMES, width), jnp.bfloat16)
    forward_recv = backward_recv = idle

    half = sections // 2
    crossed = {}
    for tick in range(turn + ticks + 1):
        back = tick - turn
        if tick < ticks:
            block, stash = forward_call(
                tick, sections, info, forward_recv, subs, weight, taps, gain, stash
            )
            pairs = [(s, s + 1) for s in range(sections - 1) if 0 <= tick - s < groups]
            forward_recv = relay(block, pairs) if pairs else idle
        if back < 0:
            continue
        block, held = backward_call(
            back, sections, info, seeds, backward_recv, crossed.get(back - 2, idle),
            weight, taps, gain, stash, held,
        )
        active = [
            s
            for s in range(1, sections)
            if 0 <= back - (sections - 1 - s) - (1 if s < half else 0) < groups
        ]
        pairs = [(s, s - 1) for s in active if s != half]
        backward_recv = relay(block, pairs) if pairs else idle
        if half in active:
            crossed[back] = relay(block, [(half, half - 1)])
        if groups <= back < ticks:
            sums = taps_call(back, sections, info, held, stash, gain, sums)

    def last_sums():
        return taps_call(ticks, sections, info, held, stash, gain, sums)

    weight_sum, taps_sums, gain_sum = column_sum(info, stash[3], held[0], last_sums, shards)
    return (weight_sum[None], jnp.transpose(taps_sums, (1, 0, 2)), gain_sum)


def solution(mesh):
    return jax.shard_map(
        body,
        mesh=mesh,
        in_specs=(
            P("dp", None),
            P("dp"),
            P(),
            P("section", None, None),
            P("section", None, None),
            P("section", None),
            P("dp", None),
        ),
        out_specs=(P("section", None, None), P("section", None, None), P("section", None)),
        check_vma=False,
    )
```

```python
import functools
import jax
import jax.numpy as jnp
from jax import lax
from jax.experimental import pallas as pl
from jax.experimental.pallas import tpu as pltpu
from jax.sharding import PartitionSpec as P

FRAMES = 96
EPS = 1e-05
LANES = 128
PAD = 16
TAPS = 31
BLOCK = 256
VMEM = 16 * 2**20


def taps_sum(padded, taps, cols, reverse):
    total = None
    for low in range(8):
        shifted = padded[pl.ds(low, FRAMES + 24), :]
        for high in range(4):
            j = 8 * high + low - 1
            if 0 <= j < TAPS:
                row = TAPS - 1 - j if reverse else j
                term = taps[row, :, cols] * shifted[8 * high : 8 * high + FRAMES]
                total = term if total is None else total + term
    return total


def lane_tile(tile):
    return pl.ds(pl.multiple_of(tile * LANES, LANES), LANES)


def lane_block(chunk):
    return pl.ds(pl.multiple_of(chunk * BLOCK, BLOCK), BLOCK)


def clear_rims(padded):
    rim = jnp.zeros((padded.shape[0], PAD, LANES), jnp.float32)
    padded[:, 0:PAD, :] = rim
    padded[:, PAD + FRAMES :, :] = rim


def frame_rows(length):
    rows = lax.broadcasted_iota(jnp.int32, (FRAMES, LANES), 0)
    return (rows < length).astype(jnp.float32)


def forward_kernel(tick, sections, info, recv, subs, weight, taps, gain, *rest):
    out, conv_all, norm_all, inv_all, hid_all, block_in, padded, total = rest[-8:]
    section = info[0]
    slot = tick - section
    width = out.shape[1]
    tiles = width // LANES
    chunks = width // BLOCK
    zeros = jnp.zeros((FRAMES, LANES), jnp.float32)

    @pl.when((slot >= 0) & (slot < subs.shape[0]))
    def _():
        @pl.when(section == 0)
        def _():
            block_in[...] = subs[slot]

        @pl.when(section != 0)
        def _():
            block_in[...] = recv[...]

        clear_rims(padded)
        mask = frame_rows(info[1 + slot])

        def add_up(tile, sums):
            return sums + block_in[:, lane_tile(tile)].astype(jnp.float32)

        centre = jnp.sum(lax.fori_loop(0, tiles, add_up, zeros, unroll=4), axis=1, keepdims=True)
        centre = jnp.broadcast_to(centre * (1.0 / width), (FRAMES, LANES))

        def add_squares(tile, sums):
            gap = block_in[:, lane_tile(tile)].astype(jnp.float32) - centre
            return sums + gap * gap

        spread = jnp.sum(
            lax.fori_loop(0, tiles, add_squares, zeros, unroll=4), axis=1, keepdims=True
        )
        inv_std = jnp.broadcast_to(lax.rsqrt(spread * (1.0 / width) + EPS), (FRAMES, LANES))
        inv_all[slot] = inv_std
        total[...] = block_in[...].astype(jnp.float32)
        hid_all[slot, :, 0:BLOCK] = jnp.zeros((FRAMES, BLOCK), jnp.bfloat16)

        def project(chunk):
            cols = lane_block(chunk)
            total[...] += jnp.dot(
                hid_all[slot, :, cols], weight[cols, :], preferred_element_type=jnp.float32
            )

        def one_chunk(chunk):
            for step in range(BLOCK // LANES):
                cols = lane_tile(chunk * (BLOCK // LANES) + step)
                normed = (block_in[:, cols].astype(jnp.float32) - centre) * inv_std
                norm_all[slot, :, cols] = normed
                padded[step, PAD : PAD + FRAMES, :] = normed * gain[:, cols] * mask
                conv = taps_sum(padded.at[step], taps, cols, False)
                conv_all[slot, :, cols] = conv
                hid_all[slot, :, cols] = (conv / (1.0 + jnp.exp(-conv))).astype(jnp.bfloat16)

        @pl.when(section != sections - 1)
        def _():
            def with_project(chunk, carry):
                project(jnp.maximum(chunk - 1, 0))
                one_chunk(chunk)
                return carry

            lax.fori_loop(0, chunks, with_project, 0)
            project(chunks - 1)
            out[...] = total[...].astype(jnp.bfloat16)

        @pl.when(section == sections - 1)
        def _():
            def without(chunk, carry):
                one_chunk(chunk)
                return carry

            lax.fori_loop(0, chunks, without, 0)


def forward_call(tick, sections, info, recv, subs, weight, taps, gain, stash):
    groups, _, width = subs.shape
    f32, bf16 = jnp.float32, jnp.bfloat16
    shapes = (
        jax.ShapeDtypeStruct((FRAMES, width), bf16),
        jax.ShapeDtypeStruct((groups, FRAMES, width), f32),
        jax.ShapeDtypeStruct((groups, FRAMES, width), f32),
        jax.ShapeDtypeStruct((groups, FRAMES, LANES), f32),
        jax.ShapeDtypeStruct((groups, FRAMES, width), bf16),
    )
    smem = pl.BlockSpec(memory_space=pltpu.SMEM)
    vmem = pl.BlockSpec(memory_space=pltpu.VMEM)
    held = () if stash is None else tuple(stash)
    res = pl.pallas_call(
        functools.partial(forward_kernel, tick, sections),
        out_shape=shapes,
        in_specs=[smem] + [vmem] * (5 + len(held)),
        out_specs=(vmem,) * 5,
        scratch_shapes=[
            pltpu.VMEM((FRAMES, width), bf16),
            pltpu.VMEM((BLOCK // LANES, FRAMES + 2 * PAD, LANES), f32),
            pltpu.VMEM((FRAMES, width), f32),
        ],
        input_output_aliases={6 + i: 1 + i for i in range(len(held))},
        compiler_params=pltpu.CompilerParams(vmem_limit_bytes=VMEM),
        cost_estimate=pl.CostEstimate(
            flops=10**6, bytes_accessed=2**10, transcendentals=0
        ),
        name="section_forward",
    )(info, recv, subs, weight, taps, gain, *held)
    return res[0], res[1:]


def backward_kernel(tick, sections, info, seeds, recv, crossed, weight, taps, gain, conv_all, norm_all, inv_all, *rest):
    out, grad_all, gconv_all, gain_all = rest[-10:-6]
    grad_out, padded, scaled_now, ahead, mean_sum, dot_sum = rest[-6:]
    section = info[0]
    late = jnp.where(section < sections // 2, 1, 0)
    slot = tick - (sections - 1 - section) - late
    width = out.shape[1]
    tiles = width // LANES
    chunks = width // BLOCK

    groups = grad_all.shape[0]

    @pl.when((slot >= 0) & (slot < groups))
    def _():
        mask = frame_rows(info[1 + slot])

        @pl.when(section == sections - 1)
        def _():
            def seed(tile, carry):
                cols = lane_tile(tile)
                masked = seeds[slot, :, cols].astype(jnp.float32) * mask
                grad_out[:, cols] = masked.astype(jnp.bfloat16)
                return carry

            lax.fori_loop(0, tiles, seed, 0)

        @pl.when(section == sections // 2 - 1)
        def _():
            grad_out[...] = crossed[...]

        @pl.when((section != sections - 1) & (section != sections // 2 - 1))
        def _():
            grad_out[...] = recv[...]

        clear_rims(padded)
        grad_all[slot] = grad_out[...]
        mean_sum[...] = jnp.zeros((FRAMES, LANES), jnp.float32)
        dot_sum[...] = jnp.zeros((FRAMES, LANES), jnp.float32)

        def back_project(chunk):
            return lax.dot_general(
                grad_out[...],
                weight[lane_block(chunk), :],
                (((1,), (1,)), ((), ())),
                preferred_element_type=jnp.float32,
            )

        ahead[0] = back_project(0)

        def one_chunk(chunk, carry):
            grad_hidden = ahead[chunk % 2]
            ahead[(chunk + 1) % 2] = back_project(jnp.minimum(chunk + 1, chunks - 1))
            for step in range(BLOCK // LANES):
                cols = lane_tile(chunk * (BLOCK // LANES) + step)
                conv = conv_all[slot, :, cols]
                sigma = 1.0 / (1.0 + jnp.exp(-conv))
                gconv = grad_hidden[:, step * LANES : (step + 1) * LANES] * sigma * (
                    1.0 + conv * (1.0 - sigma)
                )
                gconv_all[slot, :, cols] = gconv
                padded[step, PAD : PAD + FRAMES, :] = gconv
                grad_normed = taps_sum(padded.at[step], taps, cols, True) * mask
                normed = norm_all[slot, :, cols]
                product = grad_normed * normed
                part = product[0:8]
                for row in range(8, FRAMES, 8):
                    part = part + product[row : row + 8]
                gain_all[slot, :, cols] = part
                scaled = grad_normed * gain[:, cols]
                scaled_now[:, cols] = scaled
                mean_sum[...] += scaled
                dot_sum[...] += scaled * normed
            return carry

        lax.fori_loop(0, chunks, one_chunk, 0)

        @pl.when(section != 0)
        def _():
            mean_row = jnp.sum(mean_sum[...], axis=1, keepdims=True) * (1.0 / width)
            dot_row = jnp.sum(dot_sum[...], axis=1, keepdims=True) * (1.0 / width)
            mean_row = jnp.broadcast_to(mean_row, (FRAMES, LANES))
            dot_row = jnp.broadcast_to(dot_row, (FRAMES, LANES))
            inv_std = inv_all[slot]

            def finish(tile, carry):
                cols = lane_tile(tile)
                change = inv_std * (scaled_now[:, cols] - mean_row - norm_all[slot, :, cols] * dot_row)
                out[:, cols] = (grad_out[:, cols].astype(jnp.float32) + change).astype(jnp.bfloat16)
                return carry

            lax.fori_loop(0, tiles, finish, 0, unroll=2)


def backward_call(tick, sections, info, seeds, recv, crossed, weight, taps, gain, stash, held):
    groups, _, width = stash[0].shape
    f32, bf16 = jnp.float32, jnp.bfloat16
    shapes = (
        jax.ShapeDtypeStruct((FRAMES, width), bf16),
        jax.ShapeDtypeStruct((groups, FRAMES, width), bf16),
        jax.ShapeDtypeStruct((groups, FRAMES, width), f32),
        jax.ShapeDtypeStruct((groups, 8, width), f32),
    )
    smem = pl.BlockSpec(memory_space=pltpu.SMEM)
    vmem = pl.BlockSpec(memory_space=pltpu.VMEM)
    held = () if held is None else tuple(held)
    res = pl.pallas_call(
        functools.partial(backward_kernel, tick, sections),
        out_shape=shapes,
        in_specs=[smem] + [vmem] * (9 + len(held)),
        out_specs=(vmem,) * 4,
        scratch_shapes=[
            pltpu.VMEM((FRAMES, width), bf16),
            pltpu.VMEM((BLOCK // LANES, FRAMES + 2 * PAD, LANES), f32),
            pltpu.VMEM((FRAMES, width), f32),
            pltpu.VMEM((2, FRAMES, BLOCK), f32),
            pltpu.VMEM((FRAMES, LANES), f32),
            pltpu.VMEM((FRAMES, LANES), f32),
        ],
        input_output_aliases={10 + i: 1 + i for i in range(len(held))},
        compiler_params=pltpu.CompilerParams(vmem_limit_bytes=VMEM),
        cost_estimate=pl.CostEstimate(
            flops=10**6, bytes_accessed=2**10, transcendentals=0
        ),
        name="section_backward",
    )(info, seeds, recv, crossed, weight, taps, gain, *stash[:3], *held)
    return res[0], res[1:]


def taps_kernel(tick, sections, info, gconv_all, norm_all, gain, gain_all, *rest):
    out, padded = rest[-2:]
    groups = gconv_all.shape[0]
    late = jnp.where(info[0] >= sections // 2, groups, 1)
    slot = tick - (sections - 1 - info[0]) - late
    width = out.shape[1]
    if len(rest) == 2:
        out[...] = jnp.zeros(out.shape, jnp.float32)

    @pl.when((slot >= 0) & (slot < gconv_all.shape[0]))
    def _():
        mask = frame_rows(info[1 + slot])
        clear_rims(padded)

        def one_tile(tile, carry):
            cols = lane_tile(tile)
            padded[0, PAD : PAD + FRAMES, :] = norm_all[slot, :, cols] * gain[:, cols] * mask
            grads = gconv_all[slot, :, cols]
            for low in range(8):
                shifted = padded[0, pl.ds(low, FRAMES + 24), :]
                for high in range(4):
                    j = 8 * high + low - 1
                    if 0 <= j < TAPS:
                        product = grads * shifted[8 * high : 8 * high + FRAMES]
                        part = product[0:8]
                        for row in range(8, FRAMES, 8):
                            part = part + product[row : row + 8]
                        out[j : j + 1, cols] += jnp.sum(part, axis=0, keepdims=True)
            out[TAPS : TAPS + 1, cols] += jnp.sum(gain_all[slot, :, cols], axis=0, keepdims=True)
            return carry

        lax.fori_loop(0, width // LANES, one_tile, 0)


def on_chip(kernel, name, shapes, operands, scratch=(), aliases=None, hbm_out=(), flops=10**6):
    vmem = pl.BlockSpec(memory_space=pltpu.VMEM)
    smem = pl.BlockSpec(memory_space=pltpu.SMEM)
    anywhere = pl.BlockSpec(memory_space=pl.ANY)
    aliases = aliases or {}
    return pl.pallas_call(
        kernel,
        out_shape=tuple(jax.ShapeDtypeStruct(shape, dtype) for shape, dtype in shapes),
        in_specs=[smem]
        + [anywhere if aliases.get(i + 1) in hbm_out else vmem for i in range(len(operands) - 1)],
        out_specs=tuple(anywhere if i in hbm_out else vmem for i in range(len(shapes))),
        scratch_shapes=list(scratch),
        input_output_aliases=aliases,
        compiler_params=pltpu.CompilerParams(vmem_limit_bytes=VMEM),
        cost_estimate=pl.CostEstimate(flops=flops, bytes_accessed=2**10, transcendentals=0),
        name=name,
    )(*operands)


def taps_call(tick, sections, info, held, stash, gain, sums):
    width = gain.shape[1]
    operands = (info, held[1], stash[1], gain, held[2]) + (() if sums is None else (sums,))
    return on_chip(
        functools.partial(taps_kernel, tick, sections),
        "taps_gradient",
        [((TAPS + 1, width), jnp.float32)],
        operands,
        [pltpu.VMEM((1, FRAMES + 2 * PAD, LANES), jnp.float32)],
        {} if sums is None else {5: 0},
    )[0]


EXTRA = 8


def part_kernel(own, info, hid_all, grad_all, out):
    ring, sides, cut, width = out.shape
    half = info[5] if own else 1 - info[5]
    piece = 8 * cut
    tokens = hid_all.shape[0] * FRAMES
    grads = grad_all[...].reshape(tokens, width)
    for step in range(ring * sides * cut // piece):
        start = pl.multiple_of(half * (ring * sides * cut) + step * piece, LANES)
        hidden = hid_all[:, :, pl.ds(start, piece)].reshape(tokens, piece)
        part = lax.dot_general(
            hidden, grads, (((0,), (0,)), ((), ())), preferred_element_type=jnp.float32
        )
        for i in range(piece // cut):
            block = step * (piece // cut) + i
            out[block // sides, block % sides] = part[i * cut : (i + 1) * cut].astype(jnp.bfloat16)


def ring_kernel(step, info, mine, other, sums, sums_other, *rest):
    ring, sides, cut, width = mine.shape
    core, place, side = info[5], info[6], info[7]
    ahead, behind = ring // 2, ring - 1 - ring // 2
    f32 = jnp.float32
    blank = jnp.zeros((EXTRA - 1, width), f32)

    def fill(target, owner, x, *more):
        owner = owner % ring
        total = mine[owner, x].astype(f32) + other[owner, x].astype(f32)
        index = pl.ds((core * ring + owner) * sides + x, 1)
        edge = jnp.concatenate([sums[index, :] + sums_other[index, :], blank], axis=0)
        for block in more:
            total = total + block[:cut].astype(f32)
            edge = edge + block[cut:].astype(f32)
        target[:cut] = total.astype(target.dtype)
        target[cut:] = edge.astype(target.dtype)

    if step < 0:
        for n, i in enumerate(range(1) if step == -1 else range(1, ahead)):
            fill(rest[n].at[0], place + ahead - i, 1 - side)
            fill(rest[n].at[1], place + ring - behind + i, 1 - side)
        return
    crossed, arrived = rest[0], rest[1:-2]
    up, down = rest[-2:]
    fill(up, place + ahead - step, side, crossed[0], *arrived[:1])
    fill(down, place + ring - behind + step, side, crossed[1], *arrived[1:])


def place_kernel(ring, sources, count, last, info, *rest):
    blocks = rest[:count]
    whole, edge = rest[-5:-3] if last else rest[-3:-1]
    sems = rest[-1]
    core, place, side = info[5], info[6], info[7]
    cut = blocks[0].shape[-2] - EXTRA
    copies = []
    for n, (which, i, offset, core_flip, side_flip) in enumerate(sources):
        block = blocks[which] if i is None else blocks[which].at[i]
        half = 1 - core if core_flip else core
        x = 1 - side if side_flip else side
        index = (half * ring + (place + offset + ring) % ring) * 2 + x
        start = pl.multiple_of(index * cut, cut)
        copy = pltpu.make_async_copy(
            block.at[pl.ds(0, cut)], whole.at[pl.ds(start, cut)], sems.at[n]
        )
        copy.start()
        copies.append(copy)
        edge[index] = block[cut:, :].astype(jnp.float32)
    if last:
        taps_out, gain_out = rest[-3:-1]
        for row in range(TAPS):
            taps_out[row] = edge[row, 0:1, :]
        gain_out[...] = edge[TAPS, 0:1, :]
    for copy in copies:
        copy.wait()


def place_call(info, pieces, shape, ring, held):
    blocks, sources = [], []
    for block, i, offset, core_flip, side_flip in pieces:
        which = [n for n, other in enumerate(blocks) if other is block]
        if not which:
            which = [len(blocks)]
            blocks.append(block)
        sources.append((which[0], i, offset, core_flip, side_flip))
    count = len(blocks)
    return on_chip(
        functools.partial(place_kernel, ring, sources, count, held is not None),
        "place_sums",
        [(shape, jnp.bfloat16), ((4 * ring, EXTRA, shape[1]), jnp.float32)]
        + ([((TAPS, 1, shape[1]), jnp.float32), ((1, shape[1]), jnp.float32)] if held else []),
        (info, *blocks, *(held or ())),
        [pltpu.SemaphoreType.DMA((len(sources),))],
        {count + 1: 0, count + 2: 1} if held else {},
        hbm_out=(0,),
        flops=10**6 if held else 5 * 10**9,
    )


def column_sum(info, hidden, grads, sums, shards):
    ring = shards // 4
    width = grads.shape[2]
    cut = width // shards
    rows = cut + EXTRA
    f32, bf16 = jnp.float32, jnp.bfloat16

    def along_z(block, step):
        route = []
        for d in range(shards):
            x, z, c = d // (2 * ring), (d // 2) % ring, d % 2
            route.append((d, (x * ring + (z + step) % ring) * 2 + c))
        return lax.ppermute(block, "dp", route)

    def to_core(block):
        return lax.ppermute(block, "dp", [(d, d ^ 1) for d in range(shards)])

    def to_x(block):
        return lax.ppermute(block, "dp", [(d, (d + shards // 2) % shards) for d in range(shards)])

    def part(own):
        return on_chip(
            functools.partial(part_kernel, own),
            "weight_part",
            [((ring, 2, cut, width), bf16)],
            (info, hidden, grads),
        )[0]

    other = to_core(part(False))
    sums = sums()
    sums_other = to_core(sums)
    mine = part(True)
    ahead, behind = ring // 2, ring - 1 - ring // 2
    block, pair = ((rows, width), bf16), ((2, rows, width), bf16)

    def ring_call(step, *arrived):
        shapes = [block, ((rows, width), f32) if step == ahead - 1 else block]
        return on_chip(
            functools.partial(ring_kernel, step),
            "ring_step",
            shapes if step >= 0 else [pair] * (1 if step == -1 else ahead - 1),
            (info, mine, other, sums, sums_other, *arrived),
        )

    crossed = [to_x(send) for send in (*ring_call(-1), *ring_call(-2))]
    arrived = ()
    for step in range(ahead):
        up, down = ring_call(step, crossed[step], *arrived)
        up = along_z(up, 1)
        if step < ahead - 1:
            down = along_z(down, -1)
        arrived = (up, down)
    done = (down + up.astype(f32)).astype(bf16)

    ups, downs = [done], [done]
    stacks, swaps, tags = [], [], []
    for step in range(1, ahead + 1):
        ups.append(along_z(ups[-1], 1))
        if step <= behind:
            downs.append(along_z(downs[-1], -1))
        if step > 1:
            swaps.append(to_x(stacks[-1]))
        fresh = [(-step, ups[step])] + ([(step, downs[step])] if step <= behind else [])
        if step == 1:
            fresh = [(0, done)] + fresh
        tags.append([offset for offset, _ in fresh])
        stacks.append(jnp.stack([piece for _, piece in fresh]))
    swaps.append(to_x(stacks[-1]))

    def batch(groups):
        joined = jnp.concatenate([stack for stack, _, _ in groups])
        turned = to_core(joined)
        pieces = []
        count = 0
        for stack, offsets, side_flip in groups:
            for i, offset in enumerate(offsets):
                pieces.append((stack, i, offset, False, side_flip))
                pieces.append((turned, count, offset, True, side_flip))
                count += 1
        return pieces

    early = [(stacks[i], tags[i], False) for i in range(behind)]
    early += [(swaps[i], tags[i], True) for i in range(behind - 1)]
    middle = [(stacks[behind], tags[behind], False), (swaps[behind - 1], tags[behind - 1], True)]
    late = [(swaps[behind], tags[behind], True)]
    held = place_call(info, batch(early), (width, width), ring, None)
    whole, _, taps_sums, gain_sum = place_call(
        info, batch(middle + late), (width, width), ring, held
    )
    return whole, taps_sums, gain_sum


def body(mels, lengths, sub_weight, block_weight, conv_kernel, norm_gain, cotangent):
    weight = block_weight[0]
    taps = jnp.transpose(conv_kernel, (1, 0, 2))
    gain = norm_gain
    width = cotangent.shape[1]
    groups = lengths.shape[0]
    sections = lax.axis_size("section")
    shards = lax.axis_size("dp")
    section_idx = lax.axis_index("section")
    crossing = sections // 2

    def flip(shard):
        return (shard + shards // 2) % shards

    def linear(shard, section):
        return shard * sections + section

    def relay(block, pairs):
        route = []
        for source, target in pairs:
            crossed = (source < crossing) != (target < crossing)
            for shard in range(shards):
                there = flip(shard) if crossed else shard
                route.append((linear(shard, source), linear(there, target)))
        return lax.ppermute(block, ("dp", "section"), route)

    upper = range(crossing, sections)
    lens_flipped = lax.ppermute(
        lengths,
        ("dp", "section"),
        [(linear(d, s), linear(flip(d), s)) for d in range(shards) for s in upper],
    )
    lens = jnp.where(section_idx >= crossing, lens_flipped, lengths)
    seeds = lax.ppermute(
        cotangent,
        ("dp", "section"),
        [(linear(d, sections - 1), linear(flip(d), sections - 1)) for d in range(shards)],
    ).reshape(groups, FRAMES, width)
    subs = (
        jnp.dot(
            mels.reshape(groups * FRAMES, -1), sub_weight, preferred_element_type=jnp.float32
        )
        .astype(jnp.bfloat16)
        .reshape(groups, FRAMES, width)
    )
    shard = lax.axis_index("dp")
    spot = jnp.stack([shard % 2, (shard // 2) % (shards // 4), shard // (shards // 2)])
    info = jnp.concatenate([section_idx.reshape(1), lens, spot]).astype(jnp.int32)
    turn = sections - 1
    ticks = turn + groups
    stash = held = sums = None
    idle = jnp.zeros((FRAMES, width), jnp.bfloat16)
    forward_recv = backward_recv = idle

    half = sections // 2
    crossed = {}
    for tick in range(turn + ticks + 1):
        back = tick - turn
        if tick < ticks:
            block, stash = forward_call(
                tick, sections, info, forward_recv, subs, weight, taps, gain, stash
            )
            pairs = [(s, s + 1) for s in range(sections - 1) if 0 <= tick - s < groups]
            forward_recv = relay(block, pairs) if pairs else idle
        if back < 0:
            continue
        block, held = backward_call(
            back, sections, info, seeds, backward_recv, crossed.get(back - 2, idle),
            weight, taps, gain, stash, held,
        )
        active = [
            s
            for s in range(1, sections)
            if 0 <= back - (sections - 1 - s) - (1 if s < half else 0) < groups
        ]
        pairs = [(s, s - 1) for s in active if s != half]
        backward_recv = relay(block, pairs) if pairs else idle
        if half in active:
            crossed[back] = relay(block, [(half, half - 1)])
        if groups <= back < ticks:
            sums = taps_call(back, sections, info, held, stash, gain, sums)

    def last_sums():
        return taps_call(ticks, sections, info, held, stash, gain, sums)

    weight_sum, taps_sums, gain_sum = column_sum(info, stash[3], held[0], last_sums, shards)
    return (weight_sum[None], jnp.transpose(taps_sums, (1, 0, 2)), gain_sum)


def solution(mesh):
    return jax.shard_map(
        body,
        mesh=mesh,
        in_specs=(
            P("dp", None),
            P("dp"),
            P(),
            P("section", None, None),
            P("section", None, None),
            P("section", None),
            P("dp", None),
        ),
        out_specs=(P("section", None, None), P("section", None, None), P("section", None)),
        check_vma=False,
    )
```
